32 devices in a mesh: dp: 8 (over y, x, core), expert: 4 (over z).
Axes of the slice: x: 2, y: 2, z: 4, core: 2. Of those that a mesh axis runs over, the one named last changes fastest.
Arguments:
- tokens: bfloat16 [32768, 768], P(('dp', 'expert')), may hold values from -6 to 6
- bucket: int32 [128], P(('dp', 'expert')), may hold values from 0 to 49, as said below
- image_length: int32 [128], P(('dp', 'expert')), may hold values from 256 to 1024, as said below
- routes: int32 [32768, 2], P(('dp', 'expert')), may hold values from 0 to 7, all different within a row; in each aligned block of 1024 rows (0 to 1023, 1024 to 2047, ...) at most 288 rows name the same one
- cotangent: bfloat16 [32768, 768], P(('dp', 'expert')), may hold values from -6 to 6
- w_qkv: bfloat16 [768, 2304], P(('dp', 'expert')), may hold values from -0.21875 to 0.21875
- w_out: bfloat16 [768, 768], P(('dp', 'expert')), may hold values from -0.875 to 0.875
- w_ada: bfloat16 [768, 4608], P(('dp', 'expert')), may hold values from -0.21875 to 0.21875
- b_ada: bfloat16 [4608], P(('dp', 'expert')), may hold values from -3 to 3
- w_router: bfloat16 [768, 8], P(('dp', 'expert')), may hold values from -0.15625 to 0.15625
- w_shared_in: bfloat16 [768, 3072], P(('dp', 'expert')), may hold values from -0.21875 to 0.21875
- w_shared_out: bfloat16 [3072, 768], P(('dp', 'expert')), may hold values from -0.109375 to 0.109375
- w_expert_in: bfloat16 [8, 768, 3072], P('expert'), may hold values from -0.21875 to 0.21875
- w_expert_out: bfloat16 [8, 3072, 768], P('expert'), may hold values from -0.109375 to 0.109375
Outputs:
- block_out: bfloat16 [32768, 768], P(('dp', 'expert'))
- grad_tokens: bfloat16 [32768, 768], P(('dp', 'expert'))
- grad_w_qkv: float32 [768, 2304], P('dp', 'expert')
- grad_w_out: float32 [768, 768], P('dp', 'expert')
- grad_w_ada: float32 [768, 4608], P('dp', 'expert')
- grad_b_ada: float32 [4608], P(('dp', 'expert'))
- grad_w_router: float32 [768, 8], P('dp', 'expert')
- grad_w_shared_in: float32 [768, 3072], P('dp', 'expert')
- grad_w_shared_out: float32 [3072, 768], P('dp', 'expert')
- grad_w_expert_in: float32 [8, 768, 3072], P('expert', 'dp')
- grad_w_expert_out: float32 [8, 3072, 768], P('expert', 'dp')
The draws below stay inside these ranges and needn't reach their ends.
Inputs may be any that keep to these rules, and one draw needn't show every extreme that they name: `image_length`: each group of four consecutive blocks (one device's patches) carries one value: 1024 where it is one image, 256 where it is four; both kinds occur in every draw. The four blocks of one 1024-patch image carry the same bucket. `routes`: the two experts of a patch differ; within the 1024 patches of one device no expert is named more than 288 times.
All inputs are finite; a program needn't handle non-finite values.
Results may differ from the reference program's by a relative error of at most 0.02.
Values may be sent and summed in bfloat16 or wider, within the bound.
A program may use at most 384 MiB of HBM per device.

```python
import math
import jax
import jax.numpy as jnp
import numpy as np
from jax import lax

D = 768
HEADS = 12
HEAD_DIM = 64
FF = 3072
EXPERTS = 8
LONG = 1024
SHORT = 256
CAP = 288
BUCKETS = 50
TOKENS = 32768


def long_flags(key):
    device_count = TOKENS // LONG
    flag_key = jax.random.fold_in(key, 11)
    flags = jax.random.randint(flag_key, (device_count,), 0, 2)
    first_pick = jax.random.randint(jax.random.fold_in(flag_key, 1), (), 0, device_count)
    second_pick = (first_pick + 1 + jax.random.randint(jax.random.fold_in(flag_key, 2), (), 0, device_count - 1)) % device_count
    return flags.at[first_pick].set(1).at[second_pick].set(0)


def draw_image_length(key, part):
    flags = long_flags(key)
    return jnp.repeat(jnp.where(flags == 1, LONG, SHORT), 4).astype(jnp.int32)


def draw_bucket(key, part):
    flags = long_flags(key)
    key = jax.random.fold_in(key, 5)
    device_count = TOKENS // LONG
    per_block = jax.random.randint(key, (device_count, 4), 0, BUCKETS)
    long_values = jnp.repeat(per_block[:, 0:1], 4, axis=1)
    chosen = jnp.where(flags[:, None] == 1, long_values, per_block)
    chosen = chosen.at[0, :].set(0).at[device_count - 1, :].set(BUCKETS - 1)
    return chosen.reshape(-1).astype(jnp.int32)


def levels(stream_key, extent, cuts, least, largest):
    def one(axis_at, parts):
        steps = jax.random.uniform(jax.random.fold_in(jax.random.fold_in(stream_key, 6), axis_at), (parts,), jnp.float32, least / len(cuts), largest / len(cuts))
        return jnp.repeat(jnp.exp(steps), extent[axis_at] // parts).reshape((-1,) + (1,) * (len(extent) - axis_at - 1))

    level = one(*cuts[0])
    for cut in cuts[1:]:
        level = level * one(*cut)
    return level


def assign_block(key, own, number, rows, number_of, top, limit, skew):
    ranking = jax.random.permutation(key, number_of)
    crowded, usual = shares(number_of, rows * top, limit, skew, True), shares(number_of, rows * top, limit, skew, False)
    places = jnp.arange(number_of)

    def named(tallies, turn):
        used = int((tallies > 0).sum())
        fixed = max(1, used // 4)
        shifted = fixed + (places - fixed + turn * (used - fixed)) % max(1, number_of - fixed)
        return jnp.zeros((number_of,), jnp.int32).at[ranking[jnp.where(places < fixed, places, shifted)]].set(jnp.asarray(tallies, jnp.int32))

    tallies = jnp.where(number % 4 == 0, named(crowded, number // 4), named(usual, number - number // 4 - 1))
    mixed = jax.random.permutation(jax.random.fold_in(own, 3), number_of)
    giver, sink = mixed[0:number_of // 2 * 2:2], mixed[1:number_of // 2 * 2:2]
    slack = jnp.minimum(tallies[giver] - 1, limit - tallies[sink]) // 2
    slack = jnp.where((giver == ranking[0]) | (sink == ranking[0]) | (tallies[sink] == 0), 0, jnp.maximum(slack, 0))
    shifted = jax.random.randint(jax.random.fold_in(own, 4), (number_of // 2,), 0, 1 << 20) % (slack + 1)
    tallies = tallies.at[giver].add(-shifted).at[sink].add(shifted)
    members = jnp.searchsorted(jnp.cumsum(tallies), jnp.arange(rows * top), side="right").astype(jnp.int32)
    table = members.reshape(top, rows).T
    table = table[jax.random.permutation(jax.random.fold_in(own, 1), rows)]
    turn = jax.random.randint(jax.random.fold_in(own, 2), (rows, 1), 0, top)
    return jnp.take_along_axis(table, (jnp.arange(top)[None, :] + turn) % top, axis=1)


def shares(amount, total, most, slope, full):
    weights = [(1 << 20) // math.isqrt(grade ** slope) + 1 for grade in range(1, amount + 1)]
    largest = most if full else min(most, max(-(-total // amount), total * weights[0] // sum(weights)))
    least = 1 if total - largest >= amount - 1 else 0
    counts, rest = [largest] + [least] * (amount - 1), total - largest - least * (amount - 1)
    while rest > 0:
        candidates = [i for i in range(1, amount) if counts[i] < largest] or [i for i in range(1, amount) if counts[i] < most]
        mass, remaining = sum([weights[i] for i in candidates]), rest
        for i in candidates:
            more = min(most - counts[i], max(1, remaining * weights[i] // mass), rest)
            counts[i] = counts[i] + more
            rest = rest - more
    return np.array(counts)


def noise(stream_key, dims, spread, reach, cuts=(), held_as=jnp.bfloat16):
    array = jax.random.normal(stream_key, dims, jnp.float32) * spread
    if len(cuts) > 0:
        array = levels(stream_key, dims, cuts, -0.22, 0.18) * array
    return jnp.clip(array, min=-reach, max=reach).astype(held_as)


def setup_inputs(seed: int = 0) -> dict:
    streams_of = jax.random.split(jax.random.key(seed), 15)
    tokens = noise(streams_of[0], (TOKENS, D), 1.0, 6.0, ((0, 32),))
    bucket = draw_bucket(jax.random.fold_in(streams_of[14], 71), 0)
    image_length = draw_image_length(jax.random.fold_in(streams_of[14], 71), 0)
    routes_keys = jax.random.split(jax.random.fold_in(streams_of[3], 1), TOKENS // LONG)
    routes_turns = jax.random.permutation(jax.random.fold_in(streams_of[3], 3), TOKENS // LONG)
    routes = jax.vmap(lambda own, number: assign_block(jax.random.fold_in(streams_of[3], 2), own, number, LONG, EXPERTS, 2, CAP, 1))(routes_keys, routes_turns).reshape((TOKENS, 2))
    cotangent = noise(streams_of[4], (TOKENS, D), 1.0, 6.0, ((0, 32),))
    w_qkv = noise(streams_of[5], (D, 3 * D), D ** -0.5, 0.21875, ((0, 32),))
    w_out = noise(streams_of[6], (D, D), (D // 16) ** -0.5, 0.875, ((0, 32),))
    w_ada = noise(streams_of[7], (D, 6 * D), D ** -0.5, 0.21875, ((0, 32),))
    b_ada = noise(streams_of[8], (6 * D,), 0.5, 3.0, ((0, 32),))
    w_router = noise(streams_of[9], (D, EXPERTS), 0.027, 0.15625, ((0, 32),))
    w_shared_in = noise(streams_of[10], (D, FF), D ** -0.5, 0.21875, ((0, 32),))
    w_shared_out = noise(streams_of[11], (FF, D), FF ** -0.5, 0.109375, ((0, 32),))
    w_expert_in = noise(streams_of[12], (EXPERTS, D, FF), D ** -0.5, 0.21875, ((0, 4),))
    w_expert_out = noise(streams_of[13], (EXPERTS, FF, D), FF ** -0.5, 0.109375, ((0, 4),))
    return dict(tokens=tokens, bucket=bucket, image_length=image_length, routes=routes, cotangent=cotangent, w_qkv=w_qkv, w_out=w_out, w_ada=w_ada, b_ada=b_ada, w_router=w_router, w_shared_in=w_shared_in, w_shared_out=w_shared_out, w_expert_in=w_expert_in, w_expert_out=w_expert_out)


HIGHEST = lax.Precision.HIGHEST

@jax.custom_vjp
def low(v):
    return lax.optimization_barrier(v.astype(jnp.bfloat16)).astype(jnp.float32)

@jax.custom_vjp
def low_back(v):
    return v

def low_keep(v):
    return (low(v), None)

def low_pass(kept, grad):
    return (grad,)

def back_keep(v):
    return (v, None)

def back_low(kept, grad):
    return (low(grad),)
low.defvjp(low_keep, low_pass)
low_back.defvjp(back_keep, back_low)

def matmul(left_side, right_side):
    return jnp.dot(left_side, right_side, precision=HIGHEST)

def embed(bucket):
    time_values = bucket.astype(jnp.float32) * (1000.0 / BUCKETS)
    half_width = D // 2
    frequency = jnp.exp(-math.log(10000.0) * jnp.arange(half_width, dtype=jnp.float32) / half_width)
    angles = time_values[:, None] * frequency[None, :]
    return jnp.concatenate([jnp.cos(angles), jnp.sin(angles)], axis=1)

def normed(values):
    center = values - lax.optimization_barrier(jnp.mean(values, axis=-1, keepdims=True))
    variance = lax.optimization_barrier(jnp.mean(center * center, axis=-1, keepdims=True))
    return center * lax.rsqrt(variance + 1e-06)

def expand(block_rows):
    return jnp.repeat(block_rows, SHORT, axis=0)

def dispatch_slots(routes):
    flat_routes = routes.reshape(-1).astype(jnp.int32)
    chosen_hot = (flat_routes[:, None] == jnp.arange(EXPERTS, dtype=jnp.int32)[None, :]).astype(jnp.int32)
    before = (jnp.cumsum(chosen_hot, axis=0) - chosen_hot).astype(jnp.int32)
    slot_index = (flat_routes * CAP + lax.optimization_barrier(jnp.sum(before * chosen_hot, axis=1))).astype(jnp.int32)
    slot_owner = jnp.full((EXPERTS * CAP,), 2 * LONG, jnp.int32).at[slot_index].set(jnp.arange(2 * LONG, dtype=jnp.int32))
    return (slot_index, slot_owner)

def block_forward(weights, block_item):
    w_qkv, w_out, w_ada, b_ada, w_router, w_shared_in, w_shared_out, w_expert_in, w_expert_out = weights
    tokens, bucket, image_length, routes = block_item
    condition = low(jax.nn.silu(embed(bucket)))
    modulation = matmul(condition, w_ada) + b_ada
    shift_one, scale_one, gate_one, shift_two, scale_two, gate_two = [expand(modulation[:, span_index * D:(span_index + 1) * D]) for span_index in range(6)]
    normed_one = low(normed(tokens) * (1.0 + scale_one) + shift_one)
    projected = low(low_back(matmul(normed_one, w_qkv)))
    queries = projected[:, :D].reshape(LONG, HEADS, HEAD_DIM)
    key_rows = projected[:, D:2 * D].reshape(LONG, HEADS, HEAD_DIM)
    value_rows = projected[:, 2 * D:].reshape(LONG, HEADS, HEAD_DIM)
    is_long = image_length[0] == LONG
    position = jnp.arange(LONG, dtype=jnp.int32)
    segment = jnp.where(is_long, 0, position // SHORT)
    allowed = segment[:, None] == segment[None, :]
    scores = low_back(jnp.einsum('qhd,khd->hqk', queries, key_rows, precision=HIGHEST) * HEAD_DIM ** (-0.5))
    scores = jnp.where(allowed[None, :, :], scores, -1e+30)
    row_peak = lax.optimization_barrier(jnp.max(scores, axis=-1, keepdims=True))
    exp_scores = jnp.exp(scores - row_peak)
    softmax_rows = low(exp_scores / lax.optimization_barrier(jnp.sum(exp_scores, axis=-1, keepdims=True)))
    attended = jnp.einsum('hqk,khd->qhd', softmax_rows, value_rows, precision=HIGHEST).reshape(LONG, D)
    attended = low(low_back(attended))
    branch_att = low_back(matmul(attended, w_out))
    hidden_one = tokens + gate_one * branch_att
    normed_two = low(normed(hidden_one) * (1.0 + scale_two) + shift_two)
    pre_shared = low_back(matmul(normed_two, w_shared_in))
    shared = matmul(low(jax.nn.gelu(pre_shared)), w_shared_out)
    logits = matmul(normed_two, w_router)
    choose = (routes[:, :, None] == jnp.arange(EXPERTS, dtype=jnp.int32)[None, None, :]).astype(logits.dtype)
    picked_logits = lax.optimization_barrier(jnp.sum(logits[:, None, :] * choose, axis=-1))
    gate_weights = jax.nn.softmax(picked_logits, axis=-1)
    slot_index, slot_owner = dispatch_slots(routes)
    padded = jnp.concatenate([normed_two, jnp.zeros((1, D), normed_two.dtype)], axis=0)
    dispatched = low_back(padded[slot_owner // 2]).reshape(EXPERTS, CAP, D)
    pre_expert = low_back(jnp.einsum('ecd,edf->ecf', dispatched, w_expert_in, precision=HIGHEST))
    returned = jnp.einsum('ecf,efd->ecd', low(jax.nn.gelu(pre_expert)), w_expert_out, precision=HIGHEST)
    returned = low(low_back(returned)).reshape(EXPERTS * CAP, D)
    picked = returned[slot_index.reshape(LONG, 2)]
    mixture = lax.optimization_barrier(jnp.sum(gate_weights[:, :, None] * picked, axis=1))
    branch_mlp = low_back(shared + mixture)
    return hidden_one + gate_two * branch_mlp

def reference(tokens, bucket, image_length, routes, cotangent, w_qkv, w_out, w_ada, b_ada, w_router, w_shared_in, w_shared_out, w_expert_in, w_expert_out):
    weights = tuple((weight.astype(jnp.float32) for weight in (w_qkv, w_out, w_ada, b_ada, w_router, w_shared_in, w_shared_out, w_expert_in, w_expert_out)))
    block_count = TOKENS // LONG
    tokens_all = tokens.astype(jnp.float32).reshape(block_count, LONG, D)
    bucket_all = bucket.reshape(block_count, 4)
    length_all = image_length.reshape(block_count, 4)
    routes_all = routes.reshape(block_count, LONG, 2)

    def forward(weight_set, token_set):

        def one_block(block_item):
            return block_forward(weight_set, block_item)
        return lax.map(jax.checkpoint(one_block), (token_set, bucket_all, length_all, routes_all))
    outputs, pullback = jax.vjp(forward, weights, tokens_all)
    grad_weights, grad_inputs = pullback(cotangent.astype(jnp.float32).reshape(block_count, LONG, D))
    return (outputs.reshape(TOKENS, D).astype(jnp.bfloat16), grad_inputs.reshape(TOKENS, D).astype(jnp.bfloat16), grad_weights[0], grad_weights[1], grad_weights[2], grad_weights[3], grad_weights[4], grad_weights[5], grad_weights[6], grad_weights[7], grad_weights[8])
```

```python
import math

import jax
import jax.numpy as jnp
from jax import lax
from jax.experimental import pallas as pl
from jax.experimental.pallas import tpu as pltpu
from jax.sharding import PartitionSpec as P

D = 768
HEADS = 12
HEAD_DIM = 64
EXPERTS = 8
LONG = 1024
SHORT = 256
BLOCKS = LONG // SHORT
CAP = 288
EXTRA = 16
BUCKETS = 50
PAIRS = HEADS // 2
FAR = 1e30
VMEM = 60 * 2**20

HIGHEST = lax.Precision.HIGHEST
BOTH = ("dp", "expert")
HBM = pl.BlockSpec(memory_space=pl.ANY)


def product(left_side, right_side):
    return jnp.dot(left_side, right_side, preferred_element_type=jnp.float32)


def product_nt(left_side, right_side):
    return lax.dot_general(
        left_side, right_side, (((1,), (1,)), ((), ())), preferred_element_type=jnp.float32
    )


def product_tn(left_side, right_side):
    return lax.dot_general(
        left_side, right_side, (((0,), (0,)), ((), ())), preferred_element_type=jnp.float32
    )


def embed(bucket):
    time_values = bucket.astype(jnp.float32) * (1000.0 / BUCKETS)
    half_width = D // 2
    frequency = jnp.exp(-math.log(10000.0) * jnp.arange(half_width, dtype=jnp.float32) / half_width)
    angles = time_values[:, None] * frequency[None, :]
    return jnp.concatenate([jnp.cos(angles), jnp.sin(angles)], axis=1)


def normalize(values):
    center = values - jnp.mean(values, axis=-1, keepdims=True)
    variance = jnp.mean(center * center, axis=-1, keepdims=True)
    inverse = lax.rsqrt(variance + 1e-06)
    return (center * inverse, inverse)


def norm_back(grad_hat, hat_values, inverse):
    return inverse * (
        grad_hat
        - jnp.mean(grad_hat, axis=-1, keepdims=True)
        - hat_values * jnp.mean(grad_hat * hat_values, axis=-1, keepdims=True)
    )


def expand(block_rows):
    return jnp.repeat(block_rows, SHORT, axis=0)


def block_sums(values):
    return jnp.sum(values.reshape(BLOCKS, SHORT, D), axis=1)


def split_three(values):
    first = lax.reduce_precision(values, 8, 7)
    second = lax.reduce_precision(values - first, 8, 7)
    return first, second, values - first - second


def attend_kernel(length_ref, q_ref, k_ref, v_ref, out_ref, total_ref):
    far = jnp.where(length_ref[0] == LONG, 0.0, FAR)
    lane = lax.broadcasted_iota(jnp.int32, (1, 2 * HEAD_DIM), 1)
    first = lane < HEAD_DIM
    keys, vals = k_ref[...], v_ref[...]
    zero, one = jnp.zeros_like(keys), jnp.ones_like(vals)
    key_set = (jnp.where(first, keys, zero), jnp.where(first, zero, keys))
    value_set = (jnp.where(first, vals, one), jnp.where(first, one, vals))
    for i in range(BLOCKS):
        rows = slice(i * SHORT, (i + 1) * SHORT)
        q = q_ref[rows, :] * jnp.asarray(HEAD_DIM**-0.5, jnp.bfloat16)
        outs, totals = [], []
        for h in range(2):
            scores = product_nt(q, key_set[h])
            parts = [scores[:, j * SHORT : (j + 1) * SHORT] for j in range(BLOCKS)]
            away = [0.0 if i == j else far for j in range(BLOCKS)]
            peak = None
            for part, distance in zip(parts, away):
                here = jnp.max(part, axis=1, keepdims=True) - distance
                peak = here if peak is None else jnp.maximum(peak, here)
            soft = jnp.concatenate(
                [
                    jnp.exp(part - (peak + distance)).astype(jnp.bfloat16)
                    for part, distance in zip(parts, away)
                ],
                axis=1,
            )
            mixed = product(soft, value_set[h])
            total = mixed[:, HEAD_DIM : HEAD_DIM + 1] if h == 0 else mixed[:, 0:1]
            outs.append(mixed / total)
            totals.append(peak + jnp.log(total))
        out_ref[rows, :] = jnp.where(first, outs[0], outs[1]).astype(jnp.bfloat16)
        flipped = jnp.transpose(jnp.where(first, totals[0], totals[1]))
        total_ref[0, 0:1, rows] = flipped[0:1, :]
        total_ref[0, 1:2, rows] = flipped[HEAD_DIM : HEAD_DIM + 1, :]


def attend_back_kernel(
    length_ref, q_ref, k_ref, v_ref, grad_ref, out_ref, total_ref, result_ref, sum_ref
):
    pair = pl.program_id(0)
    far = jnp.where(length_ref[0] == LONG, 0.0, FAR)
    lane = lax.broadcasted_iota(jnp.int32, (1, 2 * HEAD_DIM), 1)
    first = lane < HEAD_DIM
    place = lax.broadcasted_iota(jnp.int32, (1, LONG), 1) // SHORT
    q = q_ref[...] * jnp.asarray(HEAD_DIM**-0.5, jnp.bfloat16)
    grad, keys = grad_ref[...], k_ref[...]
    zero = jnp.zeros_like(keys)
    query_set = (jnp.where(first, q, zero), jnp.where(first, zero, q))
    grad_set = (jnp.where(first, grad, zero), jnp.where(first, zero, grad))
    key_set = (jnp.where(first, keys, zero), jnp.where(first, zero, keys))
    flipped = jnp.transpose(grad.astype(jnp.float32) * out_ref[...].astype(jnp.float32))
    deltas = (
        jnp.sum(flipped[:HEAD_DIM], axis=0, keepdims=True),
        jnp.sum(flipped[HEAD_DIM:], axis=0, keepdims=True),
    )
    lanes = pl.ds(pl.multiple_of(pair * 2 * HEAD_DIM, 2 * HEAD_DIM), 2 * HEAD_DIM)
    lanes_k = pl.ds(pl.multiple_of(D + pair * 2 * HEAD_DIM, 2 * HEAD_DIM), 2 * HEAD_DIM)
    lanes_v = pl.ds(pl.multiple_of(2 * D + pair * 2 * HEAD_DIM, 2 * HEAD_DIM), 2 * HEAD_DIM)
    for j in range(BLOCKS):
        rows = slice(j * SHORT, (j + 1) * SHORT)
        key_rows, value_rows = k_ref[rows, :], v_ref[rows, :]
        grad_keys = grad_values = 0.0
        for h in range(2):
            total = total_ref[0, h : h + 1, :] + jnp.where(place == j, 0.0, far)
            soft = jnp.exp(product_nt(key_rows, query_set[h]) - total)
            grad_soft = product_nt(value_rows, grad_set[h])
            grad_scores = (soft * (grad_soft - deltas[h])).astype(jnp.bfloat16)
            grad_values += product(soft.astype(jnp.bfloat16), grad_set[h])
            grad_keys += product(grad_scores, query_set[h])
            update = product_tn(grad_scores, key_set[h][rows, :])
            if j == 0 and h == 0:
                sum_ref[...] = update
            else:
                sum_ref[...] += update
        result_ref[rows, lanes_k] = grad_keys.astype(jnp.bfloat16)
        result_ref[rows, lanes_v] = grad_values.astype(jnp.bfloat16)
    result_ref[:, lanes] = (sum_ref[...] * HEAD_DIM**-0.5).astype(jnp.bfloat16)


def column_spec(start):
    return pl.BlockSpec((LONG, 2 * HEAD_DIM), lambda pair: (0, start + pair))


def attend(image_length, projected):
    return pl.pallas_call(
        attend_kernel,
        grid=(PAIRS,),
        in_specs=[
            pl.BlockSpec(memory_space=pltpu.SMEM),
            column_spec(0),
            column_spec(PAIRS),
            column_spec(2 * PAIRS),
        ],
        out_specs=[
            column_spec(0),
            pl.BlockSpec((1, 2, LONG), lambda pair: (pair, 0, 0)),
        ],
        out_shape=[
            jax.ShapeDtypeStruct((LONG, D), jnp.bfloat16),
            jax.ShapeDtypeStruct((PAIRS, 2, LONG), jnp.float32),
        ],
        compiler_params=pltpu.CompilerParams(vmem_limit_bytes=VMEM),
        cost_estimate=pl.CostEstimate(
            flops=16 * LONG * LONG * D, bytes_accessed=8 * LONG * D, transcendentals=HEADS * LONG * LONG
        ),
        name="attend",
    )(image_length, projected, projected, projected)


def attend_back(image_length, projected, grad_attended, attended, log_total):
    return pl.pallas_call(
        attend_back_kernel,
        grid=(PAIRS,),
        in_specs=[
            pl.BlockSpec(memory_space=pltpu.SMEM),
            column_spec(0),
            column_spec(PAIRS),
            column_spec(2 * PAIRS),
            column_spec(0),
            column_spec(0),
            pl.BlockSpec((1, 2, LONG), lambda pair: (pair, 0, 0)),
        ],
        out_specs=pl.BlockSpec((LONG, 3 * D), lambda pair: (0, 0)),
        out_shape=jax.ShapeDtypeStruct((LONG, 3 * D), jnp.bfloat16),
        scratch_shapes=[pltpu.VMEM((LONG, 2 * HEAD_DIM), jnp.float32)],
        compiler_params=pltpu.CompilerParams(vmem_limit_bytes=VMEM),
        cost_estimate=pl.CostEstimate(
            flops=40 * LONG * LONG * D, bytes_accessed=16 * LONG * D, transcendentals=HEADS * LONG * LONG
        ),
        name="attend_back",
    )(image_length, projected, projected, projected, grad_attended, attended, log_total)


def turn_kernel(rows_ref, turned_ref):
    turned_ref[...] = jnp.transpose(rows_ref[...])


def turn(rows):
    count, wide = rows.shape
    return pl.pallas_call(
        turn_kernel,
        grid=(count // SHORT,),
        in_specs=[pl.BlockSpec((SHORT, wide), lambda i: (i, 0))],
        out_specs=pl.BlockSpec((wide, SHORT), lambda i: (0, i)),
        out_shape=jax.ShapeDtypeStruct((wide, count), rows.dtype),
        cost_estimate=pl.CostEstimate(flops=0, bytes_accessed=4 * count * wide, transcendentals=0),
        name="turn",
    )(rows)


def whole(shape):
    return pl.BlockSpec(shape, lambda *_: (0,) * len(shape), pipeline_mode=pl.Buffered(1))


def gelu_pair(values):
    slope, cubic = math.sqrt(2.0 / math.pi), 0.044715
    square = values * values
    gate = 0.5 + 0.5 * jnp.tanh(values * (slope + slope * cubic * square))
    result = values * gate
    return result, gate + result * (1.0 - gate) * (2.0 * slope + 6.0 * slope * cubic * square)


def ffn_step(rows_ref, grad_ref, w_in_ref, w_out_ref, gelu_ref, pre_ref, out_sum, back_sum, turned_ref, size, turn):
    step = pl.program_id(0)
    count = rows_ref.shape[0]
    w_in = w_in_ref[0]
    w_out = w_out_ref[...].reshape(w_in.shape[1], D)
    for start in range(0, count, size):
        rows = slice(start, start + size)
        pre = product(rows_ref[rows, :], w_in)
        grad_gelu = product_nt(grad_ref[rows, :], w_out)
        value, slope = gelu_pair(pre)
        value = value.astype(jnp.bfloat16)
        grad_pre = (grad_gelu * slope).astype(jnp.bfloat16)
        gelu_ref[rows, :] = value
        pre_ref[rows, :] = grad_pre
        out_sum[rows, :] += product(value, w_out)
        back_sum[rows, :] += product_nt(grad_pre, w_in)
    place = pl.ds(pl.multiple_of(jnp.minimum(step, count // turn - 1) * turn, turn), turn)
    turned_ref[:, place] = jnp.transpose(rows_ref[place, :])


def shared_kernel(rows_ref, grad_ref, w_in_ref, w_out_ref, *refs):
    out_ref, back_ref, gelu_ref, pre_ref, turned_ref = refs[-5:]

    @pl.when(pl.program_id(0) == 0)
    def _():
        out_ref[...] = jnp.zeros_like(out_ref)
        back_ref[...] = jnp.zeros_like(back_ref)

    ffn_step(
        rows_ref, grad_ref, w_in_ref, w_out_ref, gelu_ref, pre_ref, out_ref, back_ref, turned_ref, 256, 256
    )


def below(values):
    values = jnp.concatenate(
        [jnp.broadcast_to(values, (CAP, 128)), jnp.zeros((384 - CAP, 128), jnp.float32)], axis=0
    )
    values = jnp.transpose(values)[:EXTRA]
    first = values.astype(jnp.bfloat16).astype(jnp.float32)
    second = (values - first).astype(jnp.bfloat16).astype(jnp.float32)
    row = lax.broadcasted_iota(jnp.int32, values.shape, 0)
    values = jnp.where(row == 0, first, jnp.where(row == 1, second, values - first - second))
    return jnp.concatenate([values, jnp.zeros((EXTRA, D - 384), jnp.float32)], axis=1).astype(jnp.bfloat16)


def routed_kernel(senders, *refs):
    row_refs, grad_refs, refs = refs[:senders], refs[senders : 2 * senders], refs[2 * senders :]
    w_in_ref, w_out_ref = refs[:2]
    refs = refs[-2 * senders - 8 :]
    out_refs, back_refs = refs[:senders], refs[senders : 2 * senders]
    gelu_ref, pre_ref, weighted_ref, turned_ref, rows_ref, gate_ref, out_sum, back_sum = refs[2 * senders :]
    step, last = pl.program_id(0), pl.num_programs(0) - 1

    @pl.when(step == 0)
    def _():
        out_sum[...] = jnp.zeros_like(out_sum)
        back_sum[...] = jnp.zeros_like(back_sum)
        for k in range(senders):
            rows = slice(k * CAP, (k + 1) * CAP)
            rows_ref[rows, :] = row_refs[k][:CAP, :]
            pieces = row_refs[k][CAP : CAP + EXTRA, :384].astype(jnp.float32)
            gates = pieces[0:1] + pieces[1:2] + pieces[2:3]
            gate_ref[rows, :] = jnp.transpose(jnp.broadcast_to(gates, (128, 384)))[:CAP]
            weighted = gate_ref[rows, 0:1] * grad_refs[k][...].astype(jnp.float32)
            weighted_ref[rows, :] = weighted.astype(jnp.bfloat16)

    ffn_step(
        rows_ref,
        weighted_ref,
        w_in_ref,
        w_out_ref,
        gelu_ref,
        pre_ref,
        out_sum,
        back_sum,
        turned_ref,
        CAP,
        384,
    )

    @pl.when(step == last)
    def _():
        for k in range(senders):
            rows = slice(k * CAP, (k + 1) * CAP)
            result = out_sum[rows, :]
            out_refs[k][...] = (gate_ref[rows, 0:1] * result).astype(jnp.bfloat16)
            back_refs[k][:CAP, :] = back_sum[rows, :].astype(jnp.bfloat16)
            dots = jnp.sum(
                grad_refs[k][...].astype(jnp.float32) * result.astype(jnp.bfloat16).astype(jnp.float32),
                axis=1,
                keepdims=True,
            )
            back_refs[k][CAP:, :] = below(dots)


def ffn_call(kernel, name, operands, specs, w_in, w_out, place, outs, hidden, scratch, width=512, w_out_spec=None):
    ff, count = w_in.shape[2], outs[hidden].shape[0]
    column = pl.BlockSpec((count, width), lambda step: (0, step))
    out_specs = [column if at in (hidden, hidden + 1) else whole(out.shape) for at, out in enumerate(outs)]
    return pl.pallas_call(
        kernel,
        grid=(ff // width,),
        in_specs=specs
        + [
            pl.BlockSpec((1, D, width), lambda step: (place, 0, step)),
            w_out_spec or pl.BlockSpec((1, width, D), lambda step: (place, step, 0)),
        ],
        out_specs=out_specs,
        out_shape=outs,
        scratch_shapes=scratch,
        compiler_params=pltpu.CompilerParams(vmem_limit_bytes=VMEM),
        cost_estimate=pl.CostEstimate(
            flops=8 * count * D * ff, bytes_accessed=4 * count * ff + 4 * D * ff, transcendentals=count * ff
        ),
        name=name,
    )(*operands, w_in, w_out)


def shared_expert(rows, grad, w_in, w_out):
    kept = jax.ShapeDtypeStruct((LONG, D), jnp.float32)
    hidden = jax.ShapeDtypeStruct((LONG, w_in.shape[1]), jnp.bfloat16)
    turned = jax.ShapeDtypeStruct((D, LONG), jnp.bfloat16)
    full = whole((LONG, D))
    return ffn_call(
        shared_kernel,
        "shared_expert",
        [rows, grad],
        [full, full],
        w_in[None],
        w_out[0],
        0,
        [kept, kept, hidden, hidden, turned],
        2,
        [],
        D,
        w_out[1],
    )


def routed_expert(rows, grads, w_in, w_out, place):
    senders = len(rows)
    count, operands = senders * CAP, list(rows) + list(grads)
    hidden = jax.ShapeDtypeStruct((count, w_in.shape[2]), jnp.bfloat16)
    result = ffn_call(
        lambda *refs: routed_kernel(senders, *refs),
        "routed_expert",
        operands,
        [whole(operand.shape) for operand in operands],
        w_in,
        w_out,
        place,
        [jax.ShapeDtypeStruct((CAP, D), jnp.bfloat16)] * senders
        + [jax.ShapeDtypeStruct((CAP + EXTRA, D), jnp.bfloat16)] * senders
        + [
            hidden,
            hidden,
            jax.ShapeDtypeStruct((count, D), jnp.bfloat16),
            jax.ShapeDtypeStruct((D, count), jnp.bfloat16),
        ],
        2 * senders,
        [
            pltpu.VMEM((count, D), jnp.bfloat16),
            pltpu.VMEM((count, 128), jnp.float32),
            pltpu.VMEM((count, D), jnp.float32),
            pltpu.VMEM((count, D), jnp.float32),
        ],
    )
    return (result[:senders], result[senders : 2 * senders]) + tuple(result[2 * senders :])


def expert_outer_kernel(added, which_ref, gelu_ref, grad_ref, rows_ref, pre_ref, *refs):
    out_ref, step = refs[-1], pl.program_id(0)
    chips, tall = out_ref.shape[0], gelu_ref.shape[1]
    depth, count = rows_ref.shape[2:]

    @pl.when(step < chips)
    def _():
        result = product_tn(gelu_ref[...], grad_ref[...])
        if added:
            result = result + refs[0][step, :tall, :].astype(jnp.float32)
        out_ref[step, :tall, :] = result.astype(jnp.bfloat16)

    @pl.when(step >= chips)
    def _():
        result = product(rows_ref[...].reshape(chips * depth, count), pre_ref[...])
        result = result.reshape(chips, depth, D)
        place = pl.ds(pl.multiple_of(tall + (step - chips) * depth, 32), depth)
        if added:
            result = result + refs[0][:, place, :].astype(jnp.float32)
        out_ref[:, place, :] = result.astype(jnp.bfloat16)


def attention_outer_kernel(added, which_ref, normed_ref, mixed_ref, projected_ref, grad_ref, *refs):
    out_ref, step = refs[-1], pl.program_id(0)
    chips = out_ref.shape[0]
    depth, count = normed_ref.shape[2:]
    place = pl.ds(pl.multiple_of(step * depth, 32), depth)

    def put(left_ref, right_ref):
        result = product(left_ref[...].reshape(chips * depth, count), right_ref[...])
        result = result.reshape(chips, depth, D)
        if added:
            result = result + refs[0][:, place, :].astype(jnp.float32)
        out_ref[:, place, :] = result.astype(jnp.bfloat16)

    @pl.when(step < 3)
    def _():
        put(normed_ref, projected_ref)

    @pl.when(step == 3)
    def _():
        put(mixed_ref, grad_ref)


def outer_call(kernel, name, steps, which, operands, specs, rows, came, tokens, flops):
    chips = lax.axis_size("dp") // 2
    full = whole((chips, rows, D))
    extra = [] if came is None else [came]
    return pl.pallas_call(
        lambda *refs: kernel(came is not None, *refs),
        grid_spec=pltpu.PrefetchScalarGridSpec(
            num_scalar_prefetch=1,
            grid=(steps,),
            in_specs=specs + [full] * len(extra) + [HBM] * len(tokens),
            out_specs=full,
        ),
        out_shape=jax.ShapeDtypeStruct((chips, rows, D), jnp.bfloat16),
        compiler_params=pltpu.CompilerParams(vmem_limit_bytes=VMEM),
        cost_estimate=pl.CostEstimate(
            flops=flops,
            bytes_accessed=sum(2 * operand.size for operand in operands) + 4 * chips * rows * D,
            transcendentals=0,
        ),
        name=name,
    )(jnp.reshape(which, (1,)).astype(jnp.int32), *operands, *extra, *tokens)


def by_device(turned):
    n_dp = lax.axis_size("dp")
    return turned.reshape(n_dp // 2, 2, turned.shape[0] // n_dp, turned.shape[1])


def plain_outer(pairs):
    n_dp = lax.axis_size("dp")

    def make(which, came, tokens):
        parts = []
        for turned, right in pairs:
            result = product(turned, right).reshape(n_dp // 2, 2, turned.shape[0] // n_dp, right.shape[1])
            result = at_place(result, which, 1).reshape(n_dp // 2, -1, right.shape[1] // D, D)
            parts.append(jnp.swapaxes(result, 1, 2).reshape(n_dp // 2, -1, D))
        parts = jnp.concatenate(parts, axis=1)
        parts = parts if came is None else parts + came.astype(jnp.float32)
        return parts.astype(jnp.bfloat16)

    return make


def expert_outer(gelu, grad, turned, grad_pre):
    n_dp, (count, ff) = lax.axis_size("dp"), gelu.shape
    chips, tall, depth = n_dp // 2, ff // n_dp, D // n_dp
    if tall % 128 or depth % 32:
        return plain_outer([(jnp.swapaxes(gelu, 0, 1), grad), (turned, grad_pre)])
    turned = by_device(turned)
    specs = [
        pl.BlockSpec((count, tall), lambda i, which: (0, 2 * jnp.minimum(i, chips - 1) + which[0])),
        whole((count, D)),
        pl.BlockSpec((chips, 1, depth, count), lambda i, which: (0, which[0], 0, 0)),
        pl.BlockSpec((count, D), lambda i, which: (0, jnp.maximum(i - chips, 0))),
    ]
    return lambda which, came, tokens: outer_call(
        expert_outer_kernel,
        "expert_outer",
        chips + ff // D,
        which,
        [gelu, grad, turned, grad_pre],
        specs,
        tall + ff // D * depth,
        came,
        tokens,
        2 * count * D * ff,
    )


def attention_outer(left, grad_projected, grad_att):
    n_dp = lax.axis_size("dp")
    chips, depth = n_dp // 2, D // n_dp
    if depth % 32:
        return plain_outer([(left[0], grad_projected), (left[1], grad_att)])
    own = pl.BlockSpec((chips, 1, depth, LONG), lambda i, which: (0, which[0], 0, 0))
    specs = [
        own,
        own,
        pl.BlockSpec((LONG, D), lambda i, which: (0, jnp.minimum(i, 2))),
        whole((LONG, D)),
    ]
    operands = [by_device(left[0]), by_device(left[1]), grad_projected, grad_att]
    return lambda which, came, tokens: outer_call(
        attention_outer_kernel,
        "attention_outer",
        4,
        which,
        operands,
        specs,
        4 * depth,
        came,
        tokens,
        4 * LONG * D * D,
    )


def to_core(make, tokens=()):
    return make(1 - lax.axis_index("dp") % 2, None, list(tokens))


def from_core(sent):
    return lax.ppermute(sent, "dp", [(i, i ^ 1) for i in range(lax.axis_size("dp"))])


def with_core(make, came, tokens=()):
    return make(lax.axis_index("dp") % 2, came, list(tokens))


def combine_kernel(count, dotted, ids_ref, slots_ref, base_ref, *refs):
    block_refs, refs = refs[:count], refs[count:]
    out_ref, dots_out_ref, rows_ref, dots_ref = refs
    size = block_refs[0].shape[0]

    @pl.when(pl.program_id(0) == 0)
    def _():
        for at, block_ref in enumerate(block_refs):
            rows_ref[at * size : (at + 1) * size, :] = block_ref[...]
            if dotted:
                pieces = block_ref[CAP:, :size].astype(jnp.float32)
                dots_ref[:, at * size : (at + 1) * size] = pieces[0:1] + pieces[1:2] + pieces[2:3]

    ids = ids_ref[...]
    first, second = slots_ref[:, 0:1] == ids, slots_ref[:, 1:2] == ids
    hold = jnp.where(first | second, 1.0, 0.0).astype(jnp.bfloat16)
    out_ref[...] = base_ref[...] + product(hold, rows_ref[...])
    if dotted:
        dots = dots_ref[...]
        dots_out_ref[:, 0:1] = jnp.sum(jnp.where(first, dots, 0.0), axis=1, keepdims=True)
        dots_out_ref[:, 1:2] = jnp.sum(jnp.where(second, dots, 0.0), axis=1, keepdims=True)


def combine(ids, slots, base, blocks, dotted):
    total = ids.shape[1]
    patch = pl.BlockSpec((SHORT, D), lambda i: (i, 0))
    pair = pl.BlockSpec((SHORT, 2), lambda i: (i, 0))
    return pl.pallas_call(
        lambda *refs: combine_kernel(len(blocks), dotted, *refs),
        grid=(BLOCKS,),
        in_specs=[whole(ids.shape), pair, patch] + [whole(block.shape) for block in blocks],
        out_specs=[patch, pair],
        out_shape=[
            jax.ShapeDtypeStruct((LONG, D), jnp.float32),
            jax.ShapeDtypeStruct((LONG, 2), jnp.float32),
        ],
        scratch_shapes=[pltpu.VMEM((total, D), jnp.bfloat16), pltpu.VMEM((1, total), jnp.float32)],
        compiler_params=pltpu.CompilerParams(vmem_limit_bytes=VMEM),
        cost_estimate=pl.CostEstimate(
            flops=2 * LONG * total * D, bytes_accessed=2 * total * D + 8 * LONG * D, transcendentals=0
        ),
        name="combine",
    )(ids, slots, base, *blocks)


def sums_kernel(groups, *refs):
    out_ref, in_ref = refs[-2:]
    depth, wide = in_ref.shape[1:]
    expert, step = pl.program_id(0), pl.program_id(1)
    start = 0
    for at, count in enumerate(groups):
        parts = refs[start : start + count]
        start += count

        @pl.when(expert == at)
        def _(parts=parts):
            total = parts[0][...].astype(jnp.float32)
            for part in parts[1:]:
                total = total + part[...].astype(jnp.float32)

            @pl.when(step == 0)
            def _():
                out_ref[0] = total

            @pl.when(step == 1)
            def _():
                for j in range(wide // D):
                    in_ref[0, :, j * D : (j + 1) * D] = total[j * depth : (j + 1) * depth, :]


def expert_sums(pieces, tall, depth, wide):
    count = len(pieces)

    def spec(at, row):
        def index(expert, step):
            return row // tall + jnp.where(expert == at, step, 0 if at else 1), 0

        return pl.BlockSpec((tall, D), index)

    return pl.pallas_call(
        lambda *refs: sums_kernel([len(group) for group in pieces], *refs),
        grid=(count, 2),
        in_specs=[spec(at, row) for at, group in enumerate(pieces) for _, row in group],
        out_specs=[
            pl.BlockSpec((1, tall, D), lambda expert, step: (expert, 0, 0)),
            pl.BlockSpec((1, depth, wide), lambda expert, step: (expert, 0, 0)),
        ],
        out_shape=[
            jax.ShapeDtypeStruct((count, tall, D), jnp.float32),
            jax.ShapeDtypeStruct((count, depth, wide), jnp.float32),
        ],
        compiler_params=pltpu.CompilerParams(vmem_limit_bytes=VMEM),
        cost_estimate=pl.CostEstimate(
            flops=0, bytes_accessed=32 * count * tall * D, transcendentals=0
        ),
        name="expert_sums",
    )(*[array for group in pieces for array, _ in group])


def dispatch_kernel(count, ids_ref, slots_ref, gates_ref, rows_ref, *out_refs):
    size = ids_ref.shape[0] // count
    for at, out_ref in enumerate(out_refs):
        ids = ids_ref[at * size : (at + 1) * size, :]
        first, second = slots_ref[0:1, :] == ids, slots_ref[1:2, :] == ids
        hold = jnp.where(first | second, 1.0, 0.0).astype(jnp.bfloat16)
        out_ref[:CAP, :] = product(hold, rows_ref[...])[:CAP].astype(jnp.bfloat16)
        gates = jnp.where(first, gates_ref[0:1, :], 0.0) + jnp.where(second, gates_ref[1:2, :], 0.0)
        out_ref[CAP:, :] = below(jnp.sum(gates, axis=1, keepdims=True)[:CAP])


def dispatch(ids, slots, gates, rows, count):
    size = ids.shape[0] // count
    return pl.pallas_call(
        lambda *refs: dispatch_kernel(count, *refs),
        out_shape=[jax.ShapeDtypeStruct((size, D), jnp.bfloat16)] * count,
        compiler_params=pltpu.CompilerParams(vmem_limit_bytes=VMEM),
        cost_estimate=pl.CostEstimate(
            flops=2 * LONG * ids.shape[0] * D, bytes_accessed=2 * (LONG + ids.shape[0]) * D, transcendentals=0
        ),
        name="dispatch",
    )(ids, slots, gates, rows)


def gather_kernel(n_dp, n_ex, own_ref, all_ref, here_sem, z_out, z_in, chip_out, chip_in, core_out, core_in):
    dp, ex = lax.axis_index("dp"), lax.axis_index("expert")
    chips = n_dp // 2

    def along(axis, distance):
        if axis == "expert":
            return (dp, ex ^ distance)
        return (dp ^ distance, ex)

    routes = (
        [("expert", k) for k in range(1, n_ex)] + [("dp", 2 * k) for k in range(1, chips)] + [("dp", 1)]
    )
    barrier = pltpu.get_barrier_semaphore()
    for route in routes:
        pl.semaphore_signal(barrier, inc=1, device_id=along(*route), device_id_type=pl.DeviceIdType.MESH)
    pl.semaphore_wait(barrier, len(routes))

    def send(source, target, sent, came, device):
        copy = pltpu.make_async_remote_copy(
            src_ref=source,
            dst_ref=target,
            send_sem=sent,
            recv_sem=came,
            device_id=device,
            device_id_type=pl.DeviceIdType.MESH,
        )
        copy.start()
        return copy

    def wait_for(target, came):
        pltpu.make_async_remote_copy(
            src_ref=target,
            dst_ref=target,
            send_sem=came,
            recv_sem=came,
            device_id=(dp, ex),
            device_id_type=pl.DeviceIdType.MESH,
        ).wait_recv()

    def group(device, first=0, count=n_ex):
        return all_ref.at[pl.ds(device * n_ex + first, count)]

    mine = all_ref.at[dp * n_ex + ex]
    here = pltpu.make_async_copy(own_ref, mine, here_sem)
    here.start()
    sends = [
        send(own_ref, mine, z_out.at[k], z_in.at[k], along("expert", k)) for k in range(1, n_ex)
    ]
    for k in range(1, n_ex):
        wait_for(all_ref.at[dp * n_ex + (ex ^ k)], z_in.at[k])
    here.wait()
    direct = [1, 2] if chips == 4 else list(range(1, chips))
    for k in direct:
        sends.append(send(group(dp), group(dp), chip_out.at[k], chip_in.at[k], along("dp", 2 * k)))
    sends.append(send(group(dp), group(dp), core_out.at[0], core_in.at[0], along("dp", 1)))
    for k in direct:
        other = dp ^ (2 * k)
        wait_for(group(other), chip_in.at[k])
        if chips == 4:
            part = group(other, (k - 1) * (n_ex // 2), n_ex // 2)
            sends.append(send(part, part, chip_out.at[2 + k], chip_in.at[2 + k], along("dp", 2 * (3 - k))))
        sends.append(send(group(other), group(other), core_out.at[k], core_in.at[k], along("dp", 1)))
    if chips == 4:
        other = dp ^ 6
        for k in direct:
            wait_for(group(other, (k - 1) * (n_ex // 2), n_ex // 2), chip_in.at[2 + k])
        sends.append(send(group(other), group(other), core_out.at[3], core_in.at[3], along("dp", 1)))
    for k in range(chips):
        wait_for(group(dp ^ (2 * k) ^ 1), core_in.at[k])
    for copy in sends:
        copy.wait_send()


def gather(own):
    n_dp, n_ex = lax.axis_size("dp"), lax.axis_size("expert")
    chips = n_dp // 2
    counts = (n_ex, n_ex, max(chips, 5), max(chips, 5), chips, chips)
    return pl.pallas_call(
        lambda *refs: gather_kernel(n_dp, n_ex, *refs),
        in_specs=[HBM],
        out_specs=HBM,
        out_shape=jax.ShapeDtypeStruct((n_dp * n_ex,) + own.shape, own.dtype),
        scratch_shapes=[pltpu.SemaphoreType.DMA] + [pltpu.SemaphoreType.DMA((count,)) for count in counts],
        compiler_params=pltpu.CompilerParams(collective_id=0, has_side_effects=True),
        cost_estimate=pl.CostEstimate(flops=0, bytes_accessed=64 * own.size, transcendentals=0),
        name="gather",
    )(own)


def swap(parts, axis):
    return lax.all_to_all(parts, axis, 0, 0, tiled=True)


def at_place(parts, place, axis=0):
    return lax.dynamic_index_in_dim(parts, place, axis, keepdims=False)


def from_expert(parts):
    size, me = parts.shape[0], lax.axis_index("expert")
    arrived = [at_place(parts, me)]
    for distance in range(1, size):
        route = [(i, i ^ distance) for i in range(size)]
        arrived.append(lax.ppermute(at_place(parts, me ^ distance), "expert", route))
    return arrived


def together(live, work, *operands):
    def never(*operands):
        return jax.tree.map(lambda out: jnp.zeros(out.shape, out.dtype), jax.eval_shape(work, *operands))

    return lax.cond(live, work, never, *operands)


def to_expert(blocks, distances=None):
    size = len(blocks)
    return [
        lax.ppermute(blocks[distance], "expert", [(i, i ^ distance) for i in range(size)])
        if distance
        else blocks[0]
        for distance in (range(size) if distances is None else distances)
    ]


def from_chips(parts, distances):
    chips, me = lax.axis_size("dp") // 2, lax.axis_index("dp") // 2
    arrived = []
    for distance in distances if parts else []:
        route = [(i, i ^ (2 * distance)) for i in range(2 * chips)]
        part = jnp.concatenate([at_place(array, me ^ distance) for array in parts], axis=0)
        arrived.append(lax.ppermute(part, "dp", route) if distance else part)
    return arrived


def total_of(arrived):
    total = arrived[0].astype(jnp.float32)
    for part in arrived[1:]:
        total = total + part.astype(jnp.float32)
    return total


def body(
    tokens,
    bucket,
    image_length,
    routes,
    cotangent,
    w_qkv,
    w_out,
    w_ada,
    b_ada,
    w_router,
    w_shared_in,
    w_shared_out,
    w_expert_in,
    w_expert_out,
):
    n_dp, n_ex = lax.axis_size("dp"), lax.axis_size("expert")
    n, chips = n_dp * n_ex, n_dp // 2
    dp = lax.axis_index("dp")
    share = D // n
    ff = w_shared_in.shape[1]
    wide = w_ada.shape[1]
    column = wide // n

    ada_parts = jnp.swapaxes(w_ada.reshape(share, n, column), 0, 1)
    bucket_row = jnp.zeros((1, 1, column), jnp.bfloat16).at[0, 0, :BLOCKS].set(bucket.astype(jnp.bfloat16))
    ada_parts = jnp.concatenate([ada_parts, jnp.broadcast_to(bucket_row, (n, 1, column))], axis=1)
    ada_parts = swap(ada_parts, BOTH)
    ada_columns = ada_parts[:, :share].reshape(D, column)
    buckets = ada_parts[:, share, :BLOCKS].astype(jnp.int32).reshape(n * BLOCKS)
    condition = jax.nn.silu(embed(buckets)).astype(jnp.bfloat16)
    modulation = product(condition, ada_columns) + b_ada.astype(jnp.float32)
    w_qkv = w_qkv + (0.0 * modulation[0, 0]).astype(jnp.bfloat16)
    modulation = swap(modulation.reshape(n, BLOCKS, column), BOTH)
    modulation = jnp.swapaxes(modulation, 0, 1).reshape(BLOCKS, wide)

    def span(index):
        return expand(modulation[:, index * D : (index + 1) * D])

    shift_one, scale_one, gate_one, shift_two, scale_two, gate_two = [span(index) for index in range(6)]

    w_qkv = gather(w_qkv).reshape(D, 3 * D)
    router_rows = jnp.zeros((8, D), jnp.bfloat16).at[0, : share * EXPERTS].set(w_router.reshape(-1))
    packed = jnp.concatenate(
        [w_shared_out, w_out]
        + [w_shared_in[:, at * D : (at + 1) * D] for at in range(ff // D)]
        + [router_rows],
        axis=0,
    )
    packed = lax.all_gather(packed, BOTH, axis=0, tiled=False)
    start = ff // n
    w_out = packed[:, start : start + share].reshape(D, D)
    w_shared_in = jnp.concatenate(
        [
            packed[:, start + (1 + at) * share : start + (2 + at) * share].reshape(D, D)
            for at in range(ff // D)
        ],
        axis=1,
    )
    w_router = packed[:, start + (1 + ff // D) * share, : share * EXPERTS].reshape(D, EXPERTS)
    if start % 16 == 0:
        w_shared_out = packed, pl.BlockSpec((D // start, start, D), lambda step: (step, 0, 0))
    else:
        w_shared_out = packed[:, :start].reshape(1, ff, D), None

    choose = [routes[:, k : k + 1] == jnp.arange(EXPERTS, dtype=jnp.int32)[None, :] for k in range(2)]
    named = (choose[0] | choose[1]).astype(jnp.bfloat16)
    position = jnp.arange(LONG, dtype=jnp.int32)
    earlier = (position[:, None] > position[None, :]).astype(jnp.bfloat16)
    before = product(earlier, named)
    slots = [
        routes[:, k] * CAP + jnp.sum(jnp.where(choose[k], before, 0.0), axis=1).astype(jnp.int32)
        for k in range(2)
    ]
    local = EXPERTS // n_ex
    ex = lax.axis_index("expert")
    near = jnp.stack([ex ^ k for k in range(n_ex)]).astype(jnp.int32)

    def slot_ids(which, size):
        place = jnp.arange(size, dtype=jnp.int32)
        experts = jnp.asarray(which, jnp.int32)[:, None] + near[None, :] * local
        return jnp.where(place < CAP, (experts * CAP)[:, :, None] + place, -1).reshape(-1)

    def hold(at, size):
        ids = slot_ids([at], size)[:, None]
        return ((ids == slots[0][None, :]) | (ids == slots[1][None, :])).astype(jnp.bfloat16)

    slot_pairs = jnp.stack(slots, axis=1)

    grad_out = cotangent.astype(jnp.float32)
    grad_mlp = (gate_two * grad_out).astype(jnp.bfloat16)

    def grad_blocks(at, grad_mlp):
        blocks = product(hold(at, CAP), grad_mlp).astype(jnp.bfloat16).reshape(n_ex, CAP, D)
        return [blocks[k] for k in range(n_ex)]

    grad_sent = grad_blocks(0, grad_mlp)
    live = image_length[0] > 0

    inputs_full = tokens.astype(jnp.float32)
    hat_one, inverse_one = normalize(inputs_full)
    normed_one = (hat_one * (1.0 + scale_one) + shift_one).astype(jnp.bfloat16)
    projected = product(normed_one, w_qkv).astype(jnp.bfloat16)
    def attention_part(projected, blocks, grad_mlp):
        others = [grad_blocks(at, grad_mlp) for at in range(1, local)]
        return *attend(image_length, projected), to_expert(blocks), others

    attended, log_total, grad_rows, grad_sent = together(
        live, attention_part, projected, grad_sent, grad_mlp
    )
    grad_rows = [grad_rows]
    branch_att = product(attended, w_out)
    hidden_one = inputs_full + gate_one * branch_att
    hat_two, inverse_two = normalize(hidden_one)
    normed_two = (hat_two * (1.0 + scale_two) + shift_two).astype(jnp.bfloat16)

    logits = product(normed_two, w_router)
    picked_logits = jnp.stack([jnp.sum(jnp.where(pick, logits, 0.0), axis=-1) for pick in choose], axis=-1)
    gate_weights = jax.nn.softmax(picked_logits, axis=-1)
    full = CAP + EXTRA

    blocks = dispatch(
        slot_ids(range(local), full)[:, None],
        jnp.stack(slots),
        jnp.swapaxes(gate_weights, 0, 1),
        normed_two,
        local * n_ex,
    )
    sent = [blocks[at * n_ex : (at + 1) * n_ex] for at in range(local)]

    tall = ff // n_dp
    size = tall + ff // D * (D // n_dp)
    near_chips, far_chips = list(range(min(3, chips))), list(range(3, chips))

    def split_expert(part):
        blocks = jnp.swapaxes(part[tall:].reshape(ff // D, D // n_dp, D), 0, 1)
        return part[:tall], blocks.reshape(D // n_dp, ff)

    pieces = [[] for _ in range(1 + local)]

    def note(arrays, *which):
        for row, at in enumerate(which):
            pieces[at] += [(array, row * size) for array in arrays]

    def sum_of(at):
        return total_of([array[row : row + size] for array, row in pieces[at]])

    def first_part(normed_two, grad_mlp, blocks):
        results = shared_expert(normed_two, grad_mlp, w_shared_in, w_shared_out)
        half = to_core(expert_outer(results[2], grad_mlp, results[4], results[3]))
        return results, half, to_expert(blocks)

    results, shared_half, arrived = together(live, first_part, normed_two, grad_mlp, sent[0])
    shared, grad_normed_two, gelu_shared, grad_pre_shared, turned_shared = results

    def second_part(rows, grads, others):
        results = routed_expert(rows, grads, w_expert_in, w_expert_out, 0)
        half = to_core(expert_outer(results[2], results[4], results[5], results[3]))
        return results, half, [to_expert(blocks) for blocks in others]

    def weights_part(gelu, weighted, turned, grad_pre, half, shared_half, grads):
        came = [from_core(half), from_core(shared_half)]
        kept = [with_core(expert_outer(gelu, weighted, turned, grad_pre), came[0])]
        make = expert_outer(gelu_shared, grad_mlp, turned_shared, grad_pre_shared)
        kept.append(with_core(make, came[1], kept))
        return kept, [to_expert(blocks) for blocks in grads]

    results, half, others = together(live, second_part, arrived, grad_rows[0], sent[1:])
    outs, backs, gelu, grad_pre, weighted, turned_rows = results
    arrived = [arrived] + others
    (kept_first, kept_shared), others = together(
        live, weights_part, gelu, weighted, turned_rows, grad_pre, half, shared_half, grad_sent
    )
    grad_rows += others
    out_rows, grad_home, kept_last = [outs], [], []

    def third_part(rows, grads, at, backs, kept):
        results = routed_expert(rows, grads, w_expert_in, w_expert_out, at)
        half = to_core(expert_outer(results[2], results[4], results[5], results[3]))
        return results, half, to_expert(backs), from_chips(kept, near_chips)

    def fourth_part(gelu, weighted, turned, grad_pre, half, backs, kept):
        kept_now = with_core(expert_outer(gelu, weighted, turned, grad_pre), from_core(half))
        return kept_now, to_expert(backs), from_chips(kept, far_chips), [turn(normed_one), turn(attended)]

    if local == 1:
        turned = [turn(normed_one), turn(attended)]
        backs = to_expert(backs)
        note(from_chips([kept_first], near_chips), 0)
        note(from_chips([kept_shared], near_chips + far_chips), 1)
    for at in range(1, local):
        results, half, home, part = together(
            live,
            lambda rows, grads, backs, kept, at=at: third_part(rows, grads, at, backs, kept),
            arrived[at],
            grad_rows[at],
            backs,
            [kept_first, kept_shared] if at == 1 else kept_last[-1:],
        )
        note(part, *((0, 1) if at == 1 else (at,)))
        outs, backs, gelu, grad_pre, weighted, turned_rows = results
        out_rows.append(outs)
        grad_home.append(home)
        kept_now, backs, part, turned = together(
            live,
            fourth_part,
            gelu,
            weighted,
            turned_rows,
            grad_pre,
            half,
            backs,
            [kept_shared] if at == 1 else kept_last[-1:],
        )
        note(part, 1 if at == 1 else at)
        kept_last.append(kept_now)
    grad_home.append(backs)

    def fifth_part(grad_normed_two, grad_home, others, kept):
        ids = slot_ids(range(local), full)[None, :]
        grad_normed_two, grad_gates = combine(ids, slot_pairs, grad_normed_two, sum(grad_home, []), True)
        grad_picked = gate_weights * (
            grad_gates - jnp.sum(gate_weights * grad_gates, axis=1, keepdims=True)
        )
        grad_logits = jnp.where(choose[0], grad_picked[:, 0:1], 0.0) + jnp.where(
            choose[1], grad_picked[:, 1:2], 0.0
        )
        logit_parts = jnp.concatenate(split_three(grad_logits), axis=1).astype(jnp.bfloat16)
        grad_router = product_tn(normed_two, logit_parts).reshape(D, 3, EXPERTS).sum(axis=1)
        grad_normed_two = grad_normed_two + product_nt(
            logit_parts, jnp.concatenate([w_router, w_router, w_router], axis=1)
        )

        grad_hidden_one = cotangent.astype(jnp.float32) + norm_back(
            grad_normed_two * (1.0 + span(4)), hat_two, inverse_two
        )
        grad_att = (span(2) * grad_hidden_one).astype(jnp.bfloat16)
        grad_attended = product_nt(grad_att, w_out).astype(jnp.bfloat16)
        grad_spans = [
            block_sums(grad_hidden_one * product(attended, w_out)),
            block_sums(grad_normed_two),
            block_sums(grad_normed_two * hat_two),
        ]
        results = (grad_router, grad_spans, grad_hidden_one, grad_att, grad_attended)
        return results, [to_expert(blocks) for blocks in others], from_chips(kept, near_chips)

    results, returned, part = together(
        live, fifth_part, grad_normed_two, grad_home, out_rows[:-1], kept_last[-1:]
    )
    grad_router, grad_spans, grad_hidden_one, grad_att, grad_attended = results
    note(part, local)

    def sixth_part(projected, grad_attended, attended, log_total, blocks, kept):
        result = attend_back(image_length, projected, grad_attended, attended, log_total)
        half = to_core(attention_outer(turned, result, grad_att))
        grad_shared_out, grad_shared_in = split_expert(sum_of(1).astype(jnp.bfloat16))
        rows = (D // n_dp) * (ff // n_ex) // D
        shared_parts = jnp.concatenate(
            [
                jnp.swapaxes(grad_shared_in.reshape(D // n_dp, n_ex, ff // n_ex), 0, 1).reshape(
                    n_ex, rows, D
                ),
                jnp.swapaxes(grad_shared_out.reshape(ff // n_dp, n_ex, D // n_ex), 0, 1).reshape(
                    n_ex, rows, D
                ),
            ],
            axis=1,
        )
        return result, half, to_expert(blocks), from_chips(kept, far_chips), shared_parts

    grad_projected, half, rows, part, shared_parts = together(
        live,
        sixth_part,
        projected,
        grad_attended,
        attended,
        log_total,
        out_rows[-1],
        [kept_first] + kept_last[-1:],
    )
    note(part, *([0, local] if local > 1 else [0]))
    returned.append(rows)

    def seventh_part(grad_projected, half, shared_parts):
        came = from_core(half)
        grad_normed_one = product_nt(grad_projected, w_qkv)
        hat_one, inverse_one = normalize(tokens.astype(jnp.float32))
        grad_input = grad_hidden_one + norm_back(
            grad_normed_one * (1.0 + span(1)), hat_one, inverse_one
        )
        spans = [block_sums(grad_normed_one), block_sums(grad_normed_one * hat_one)]
        kept = with_core(attention_outer(turned, grad_projected, grad_att), came)
        return grad_input.astype(jnp.bfloat16), spans, kept, from_expert(shared_parts)

    grad_input, spans, kept, shared_parts = together(
        live, seventh_part, grad_projected, half, shared_parts
    )

    def eighth_part(kept, returned):
        arrived = from_chips([kept], list(range(chips)))
        routed = [group for at, group in enumerate(pieces) if at != 1]
        grad_expert_out, grad_expert_in = expert_sums(routed, tall, D // n_dp, ff)
        ids = slot_ids(range(local), CAP)[None, :]
        branch_mlp = combine(ids, slot_pairs, shared, sum(returned, []), False)[0]
        result = hidden_one + span(5) * branch_mlp
        last_span = block_sums(cotangent.astype(jnp.float32) * branch_mlp)
        return arrived, grad_expert_out, grad_expert_in, result.astype(jnp.bfloat16), last_span

    attention_parts, grad_expert_out, grad_expert_in, result, last_span = together(
        live, eighth_part, kept, returned
    )
    grad_modulation = jnp.concatenate(spans + grad_spans + [last_span], axis=1)

    own_wide, router_rows, router_columns = wide // n_ex, D // n_dp, EXPERTS // n_ex
    by_expert = jnp.swapaxes(grad_modulation.reshape(BLOCKS, n_ex, own_wide), 0, 1)
    message = jnp.concatenate(
        [
            jnp.broadcast_to(
                by_expert.reshape(1, n_ex, BLOCKS * own_wide), (n_dp, n_ex, BLOCKS * own_wide)
            ),
            jnp.sum(grad_modulation, axis=0).reshape(n_dp, n_ex, column),
            jnp.swapaxes(grad_router.reshape(n_dp, router_rows, n_ex, router_columns), 1, 2).reshape(
                n_dp, n_ex, router_rows * router_columns
            ),
        ],
        axis=2,
    )
    length = message.shape[2]
    message = jnp.pad(message, ((0, 0), (0, 0), (0, -length % 128))).reshape(n, -1, 128)
    message = swap(message, BOTH).reshape(n, -1)
    at = BLOCKS * own_wide
    every_modulation = message[:, :at].reshape(n * BLOCKS, own_wide)
    grad_b_ada = jnp.sum(message[:, at : at + column], axis=0)
    grad_router = jnp.sum(message[:, at + column : length], axis=0).reshape(router_rows, router_columns)
    own_condition = lax.dynamic_slice_in_dim(condition, dp * (D // n_dp), D // n_dp, axis=1)

    attention_parts = total_of(attention_parts).astype(jnp.bfloat16).reshape(4, D // n_dp, D)
    attention_parts = jnp.concatenate(
        [
            jnp.swapaxes(attention_parts[:3], 0, 1).reshape(D // n_dp, n_ex, 3 * D // n_ex),
            attention_parts[3].reshape(D // n_dp, n_ex, D // n_ex),
        ],
        axis=2,
    )
    rest = (D // n_dp) * 4 // n_ex
    attention_parts = jnp.swapaxes(attention_parts, 0, 1).reshape(n_ex, rest, D)

    parts = together(live, from_expert, attention_parts)
    grad_w_ada = lax.dot_general(
        own_condition.astype(jnp.float32),
        every_modulation,
        (((0,), (0,)), ((), ())),
        precision=HIGHEST,
        preferred_element_type=jnp.float32,
    )
    attention_parts = total_of(parts).reshape(D // n_dp, 4 * D // n_ex)
    shared_parts = total_of(shared_parts)
    half = shared_parts.shape[0] // 2
    return (
        result,
        grad_input,
        attention_parts[:, : 3 * D // n_ex],
        attention_parts[:, 3 * D // n_ex :],
        grad_w_ada,
        grad_b_ada,
        grad_router,
        shared_parts[:half].reshape(D // n_dp, ff // n_ex),
        shared_parts[half:].reshape(ff // n_dp, D // n_ex),
        grad_expert_in,
        grad_expert_out,
    )


def solution(mesh):
    rows, flat = P(BOTH, None), P(BOTH)
    spread = P("dp", "expert")
    return jax.shard_map(
        body,
        mesh=mesh,
        in_specs=(
            rows,
            flat,
            flat,
            rows,
            rows,
            rows,
            rows,
            rows,
            flat,
            rows,
            rows,
            rows,
            P("expert", None, None),
            P("expert", None, None),
        ),
        out_specs=(
            rows,
            rows,
            spread,
            spread,
            spread,
            flat,
            spread,
            spread,
            spread,
            P("expert", "dp", None),
            P("expert", "dp", None),
        ),
        check_vma=False,
    )
```

```python
import math

import jax
import jax.numpy as jnp
from jax import lax
from jax.experimental import pallas as pl
from jax.experimental.pallas import tpu as pltpu
from jax.sharding import PartitionSpec as P

D = 768
HEADS = 12
HEAD_DIM = 64
EXPERTS = 8
LONG = 1024
SHORT = 256
BLOCKS = LONG // SHORT
CAP = 288
EXTRA = 16
BUCKETS = 50
PAIRS = HEADS // 2
FAR = 1e30
VMEM = 60 * 2**20

HIGHEST = lax.Precision.HIGHEST
BOTH = ("dp", "expert")
HBM = pl.BlockSpec(memory_space=pl.ANY)


def product(left_side, right_side):
    return jnp.dot(left_side, right_side, preferred_element_type=jnp.float32)


def product_nt(left_side, right_side):
    return lax.dot_general(
        left_side, right_side, (((1,), (1,)), ((), ())), preferred_element_type=jnp.float32
    )


def product_tn(left_side, right_side):
    return lax.dot_general(
        left_side, right_side, (((0,), (0,)), ((), ())), preferred_element_type=jnp.float32
    )


def embed(bucket):
    time_values = bucket.astype(jnp.float32) * (1000.0 / BUCKETS)
    half_width = D // 2
    frequency = jnp.exp(-math.log(10000.0) * jnp.arange(half_width, dtype=jnp.float32) / half_width)
    angles = time_values[:, None] * frequency[None, :]
    return jnp.concatenate([jnp.cos(angles), jnp.sin(angles)], axis=1)


def normalize(values):
    center = values - jnp.mean(values, axis=-1, keepdims=True)
    variance = jnp.mean(center * center, axis=-1, keepdims=True)
    inverse = lax.rsqrt(variance + 1e-06)
    return (center * inverse, inverse)


def norm_back(grad_hat, hat_values, inverse):
    return inverse * (
        grad_hat
        - jnp.mean(grad_hat, axis=-1, keepdims=True)
        - hat_values * jnp.mean(grad_hat * hat_values, axis=-1, keepdims=True)
    )


def expand(block_rows):
    return jnp.repeat(block_rows, SHORT, axis=0)


def block_sums(values):
    return jnp.sum(values.reshape(BLOCKS, SHORT, D), axis=1)


def split_three(values):
    first = lax.reduce_precision(values, 8, 7)
    second = lax.reduce_precision(values - first, 8, 7)
    return first, second, values - first - second


def attend_kernel(length_ref, q_ref, k_ref, v_ref, out_ref, total_ref):
    far = jnp.where(length_ref[0] == LONG, 0.0, FAR)
    lane = lax.broadcasted_iota(jnp.int32, (1, 2 * HEAD_DIM), 1)
    first = lane < HEAD_DIM
    keys, vals = k_ref[...], v_ref[...]
    zero, one = jnp.zeros_like(keys), jnp.ones_like(vals)
    key_set = (jnp.where(first, keys, zero), jnp.where(first, zero, keys))
    value_set = (jnp.where(first, vals, one), jnp.where(first, one, vals))
    for i in range(BLOCKS):
        rows = slice(i * SHORT, (i + 1) * SHORT)
        q = q_ref[rows, :] * jnp.asarray(HEAD_DIM**-0.5, jnp.bfloat16)
        outs, totals = [], []
        for h in range(2):
            scores = product_nt(q, key_set[h])
            parts = [scores[:, j * SHORT : (j + 1) * SHORT] for j in range(BLOCKS)]
            away = [0.0 if i == j else far for j in range(BLOCKS)]
            peak = None
            for part, distance in zip(parts, away):
                here = jnp.max(part, axis=1, keepdims=True) - distance
                peak = here if peak is None else jnp.maximum(peak, here)
            soft = jnp.concatenate(
                [
                    jnp.exp(part - (peak + distance)).astype(jnp.bfloat16)
                    for part, distance in zip(parts, away)
                ],
                axis=1,
            )
            mixed = product(soft, value_set[h])
            total = mixed[:, HEAD_DIM : HEAD_DIM + 1] if h == 0 else mixed[:, 0:1]
            outs.append(mixed / total)
            totals.append(peak + jnp.log(total))
        out_ref[rows, :] = jnp.where(first, outs[0], outs[1]).astype(jnp.bfloat16)
        flipped = jnp.transpose(jnp.where(first, totals[0], totals[1]))
        total_ref[0, 0:1, rows] = flipped[0:1, :]
        total_ref[0, 1:2, rows] = flipped[HEAD_DIM : HEAD_DIM + 1, :]


def attend_back_kernel(
    length_ref, q_ref, k_ref, v_ref, grad_ref, out_ref, total_ref, result_ref, sum_ref
):
    pair = pl.program_id(0)
    far = jnp.where(length_ref[0] == LONG, 0.0, FAR)
    lane = lax.broadcasted_iota(jnp.int32, (1, 2 * HEAD_DIM), 1)
    first = lane < HEAD_DIM
    place = lax.broadcasted_iota(jnp.int32, (1, LONG), 1) // SHORT
    q = q_ref[...] * jnp.asarray(HEAD_DIM**-0.5, jnp.bfloat16)
    grad, keys = grad_ref[...], k_ref[...]
    zero = jnp.zeros_like(keys)
    query_set = (jnp.where(first, q, zero), jnp.where(first, zero, q))
    grad_set = (jnp.where(first, grad, zero), jnp.where(first, zero, grad))
    key_set = (jnp.where(first, keys, zero), jnp.where(first, zero, keys))
    flipped = jnp.transpose(grad.astype(jnp.float32) * out_ref[...].astype(jnp.float32))
    deltas = (
        jnp.sum(flipped[:HEAD_DIM], axis=0, keepdims=True),
        jnp.sum(flipped[HEAD_DIM:], axis=0, keepdims=True),
    )
    lanes = pl.ds(pl.multiple_of(pair * 2 * HEAD_DIM, 2 * HEAD_DIM), 2 * HEAD_DIM)
    lanes_k = pl.ds(pl.multiple_of(D + pair * 2 * HEAD_DIM, 2 * HEAD_DIM), 2 * HEAD_DIM)
    lanes_v = pl.ds(pl.multiple_of(2 * D + pair * 2 * HEAD_DIM, 2 * HEAD_DIM), 2 * HEAD_DIM)
    for j in range(BLOCKS):
        rows = slice(j * SHORT, (j + 1) * SHORT)
        key_rows, value_rows = k_ref[rows, :], v_ref[rows, :]
        grad_keys = grad_values = 0.0
        for h in range(2):
            total = total_ref[0, h : h + 1, :] + jnp.where(place == j, 0.0, far)
            soft = jnp.exp(product_nt(key_rows, query_set[h]) - total)
            grad_soft = product_nt(value_rows, grad_set[h])
            grad_scores = (soft * (grad_soft - deltas[h])).astype(jnp.bfloat16)
            grad_values += product(soft.astype(jnp.bfloat16), grad_set[h])
            grad_keys += product(grad_scores, query_set[h])
            update = product_tn(grad_scores, key_set[h][rows, :])
            if j == 0 and h == 0:
                sum_ref[...] = update
            else:
                sum_ref[...] += update
        result_ref[rows, lanes_k] = grad_keys.astype(jnp.bfloat16)
        result_ref[rows, lanes_v] = grad_values.astype(jnp.bfloat16)
    result_ref[:, lanes] = (sum_ref[...] * HEAD_DIM**-0.5).astype(jnp.bfloat16)


def column_spec(start):
    return pl.BlockSpec((LONG, 2 * HEAD_DIM), lambda pair: (0, start + pair))


def attend(image_length, projected):
    return pl.pallas_call(
        attend_kernel,
        grid=(PAIRS,),
        in_specs=[
            pl.BlockSpec(memory_space=pltpu.SMEM),
            column_spec(0),
            column_spec(PAIRS),
            column_spec(2 * PAIRS),
        ],
        out_specs=[
            column_spec(0),
            pl.BlockSpec((1, 2, LONG), lambda pair: (pair, 0, 0)),
        ],
        out_shape=[
            jax.ShapeDtypeStruct((LONG, D), jnp.bfloat16),
            jax.ShapeDtypeStruct((PAIRS, 2, LONG), jnp.float32),
        ],
        compiler_params=pltpu.CompilerParams(vmem_limit_bytes=VMEM),
        cost_estimate=pl.CostEstimate(
            flops=16 * LONG * LONG * D, bytes_accessed=8 * LONG * D, transcendentals=HEADS * LONG * LONG
        ),
        name="attend",
    )(image_length, projected, projected, projected)


def attend_back(image_length, projected, grad_attended, attended, log_total):
    return pl.pallas_call(
        attend_back_kernel,
        grid=(PAIRS,),
        in_specs=[
            pl.BlockSpec(memory_space=pltpu.SMEM),
            column_spec(0),
            column_spec(PAIRS),
            column_spec(2 * PAIRS),
            column_spec(0),
            column_spec(0),
            pl.BlockSpec((1, 2, LONG), lambda pair: (pair, 0, 0)),
        ],
        out_specs=pl.BlockSpec((LONG, 3 * D), lambda pair: (0, 0)),
        out_shape=jax.ShapeDtypeStruct((LONG, 3 * D), jnp.bfloat16),
        scratch_shapes=[pltpu.VMEM((LONG, 2 * HEAD_DIM), jnp.float32)],
        compiler_params=pltpu.CompilerParams(vmem_limit_bytes=VMEM),
        cost_estimate=pl.CostEstimate(
            flops=40 * LONG * LONG * D, bytes_accessed=16 * LONG * D, transcendentals=HEADS * LONG * LONG
        ),
        name="attend_back",
    )(image_length, projected, projected, projected, grad_attended, attended, log_total)


def turn_kernel(rows_ref, turned_ref):
    turned_ref[...] = jnp.transpose(rows_ref[...])


def turn(rows):
    count, wide = rows.shape
    return pl.pallas_call(
        turn_kernel,
        grid=(count // SHORT,),
        in_specs=[pl.BlockSpec((SHORT, wide), lambda i: (i, 0))],
        out_specs=pl.BlockSpec((wide, SHORT), lambda i: (0, i)),
        out_shape=jax.ShapeDtypeStruct((wide, count), rows.dtype),
        cost_estimate=pl.CostEstimate(flops=0, bytes_accessed=4 * count * wide, transcendentals=0),
        name="turn",
    )(rows)


def whole(shape):
    return pl.BlockSpec(shape, lambda *_: (0,) * len(shape), pipeline_mode=pl.Buffered(1))


def gelu_pair(values):
    slope, cubic = math.sqrt(2.0 / math.pi), 0.044715
    square = values * values
    gate = 0.5 + 0.5 * jnp.tanh(values * (slope + slope * cubic * square))
    result = values * gate
    return result, gate + result * (1.0 - gate) * (2.0 * slope + 6.0 * slope * cubic * square)


def ffn_step(rows_ref, grad_ref, w_in_ref, w_out_ref, gelu_ref, pre_ref, out_sum, back_sum, turned_ref, size, turn):
    step = pl.program_id(0)
    count = rows_ref.shape[0]
    w_in = w_in_ref[0]
    w_out = w_out_ref[...].reshape(w_in.shape[1], D)
    for start in range(0, count, size):
        rows = slice(start, start + size)
        pre = product(rows_ref[rows, :], w_in)
        grad_gelu = product_nt(grad_ref[rows, :], w_out)
        value, slope = gelu_pair(pre)
        value = value.astype(jnp.bfloat16)
        grad_pre = (grad_gelu * slope).astype(jnp.bfloat16)
        gelu_ref[rows, :] = value
        pre_ref[rows, :] = grad_pre
        out_sum[rows, :] += product(value, w_out)
        back_sum[rows, :] += product_nt(grad_pre, w_in)
    place = pl.ds(pl.multiple_of(jnp.minimum(step, count // turn - 1) * turn, turn), turn)
    turned_ref[:, place] = jnp.transpose(rows_ref[place, :])


def shared_kernel(rows_ref, grad_ref, w_in_ref, w_out_ref, *refs):
    out_ref, back_ref, gelu_ref, pre_ref, turned_ref = refs[-5:]

    @pl.when(pl.program_id(0) == 0)
    def _():
        out_ref[...] = jnp.zeros_like(out_ref)
        back_ref[...] = jnp.zeros_like(back_ref)

    ffn_step(
        rows_ref, grad_ref, w_in_ref, w_out_ref, gelu_ref, pre_ref, out_ref, back_ref, turned_ref, 256, 256
    )


def below(values):
    values = jnp.concatenate(
        [jnp.broadcast_to(values, (CAP, 128)), jnp.zeros((384 - CAP, 128), jnp.float32)], axis=0
    )
    values = jnp.transpose(values)[:EXTRA]
    first = values.astype(jnp.bfloat16).astype(jnp.float32)
    second = (values - first).astype(jnp.bfloat16).astype(jnp.float32)
    row = lax.broadcasted_iota(jnp.int32, values.shape, 0)
    values = jnp.where(row == 0, first, jnp.where(row == 1, second, values - first - second))
    return jnp.concatenate([values, jnp.zeros((EXTRA, D - 384), jnp.float32)], axis=1).astype(jnp.bfloat16)


def routed_kernel(senders, *refs):
    row_refs, grad_refs, refs = refs[:senders], refs[senders : 2 * senders], refs[2 * senders :]
    w_in_ref, w_out_ref = refs[:2]
    refs = refs[-2 * senders - 8 :]
    out_refs, back_refs = refs[:senders], refs[senders : 2 * senders]
    gelu_ref, pre_ref, weighted_ref, turned_ref, rows_ref, gate_ref, out_sum, back_sum = refs[2 * senders :]
    step, last = pl.program_id(0), pl.num_programs(0) - 1

    @pl.when(step == 0)
    def _():
        out_sum[...] = jnp.zeros_like(out_sum)
        back_sum[...] = jnp.zeros_like(back_sum)
        for k in range(senders):
            rows = slice(k * CAP, (k + 1) * CAP)
            rows_ref[rows, :] = row_refs[k][:CAP, :]
            pieces = row_refs[k][CAP : CAP + EXTRA, :384].astype(jnp.float32)
            gates = pieces[0:1] + pieces[1:2] + pieces[2:3]
            gate_ref[rows, :] = jnp.transpose(jnp.broadcast_to(gates, (128, 384)))[:CAP]
            weighted = gate_ref[rows, 0:1] * grad_refs[k][...].astype(jnp.float32)
            weighted_ref[rows, :] = weighted.astype(jnp.bfloat16)

    ffn_step(
        rows_ref,
        weighted_ref,
        w_in_ref,
        w_out_ref,
        gelu_ref,
        pre_ref,
        out_sum,
        back_sum,
        turned_ref,
        CAP,
        384,
    )

    @pl.when(step == last)
    def _():
        for k in range(senders):
            rows = slice(k * CAP, (k + 1) * CAP)
            result = out_sum[rows, :]
            out_refs[k][...] = (gate_ref[rows, 0:1] * result).astype(jnp.bfloat16)
            back_refs[k][:CAP, :] = back_sum[rows, :].astype(jnp.bfloat16)
            dots = jnp.sum(
                grad_refs[k][...].astype(jnp.float32) * result.astype(jnp.bfloat16).astype(jnp.float32),
                axis=1,
                keepdims=True,
            )
            back_refs[k][CAP:, :] = below(dots)


def ffn_call(kernel, name, operands, specs, w_in, w_out, place, outs, hidden, scratch, width=512, w_specs=None):
    count, ff = outs[hidden].shape
    column = pl.BlockSpec((count, width), lambda step: (0, step))
    out_specs = [column if at in (hidden, hidden + 1) else whole(out.shape) for at, out in enumerate(outs)]
    return pl.pallas_call(
        kernel,
        grid=(ff // width,),
        in_specs=specs
        + (
            w_specs
            or [
                pl.BlockSpec((1, D, width), lambda step: (place, 0, step)),
                pl.BlockSpec((1, width, D), lambda step: (place, step, 0)),
            ]
        ),
        out_specs=out_specs,
        out_shape=outs,
        scratch_shapes=scratch,
        compiler_params=pltpu.CompilerParams(vmem_limit_bytes=VMEM),
        cost_estimate=pl.CostEstimate(
            flops=8 * count * D * ff, bytes_accessed=4 * count * ff + 4 * D * ff, transcendentals=count * ff
        ),
        name=name,
    )(*operands, w_in, w_out)


def shared_expert(rows, grad, w_in, w_out):
    kept = jax.ShapeDtypeStruct((LONG, D), jnp.float32)
    hidden = jax.ShapeDtypeStruct((LONG, w_in.shape[0] * D), jnp.bfloat16)
    turned = jax.ShapeDtypeStruct((D, LONG), jnp.bfloat16)
    full = whole((LONG, D))
    return ffn_call(
        shared_kernel,
        "shared_expert",
        [rows, grad],
        [full, full],
        w_in,
        w_out[0],
        0,
        [kept, kept, hidden, hidden, turned],
        2,
        [],
        D,
        [
            pl.BlockSpec((1, D, D), lambda step: (step, 0, 0)),
            w_out[1] or pl.BlockSpec((1, D, D), lambda step: (0, step, 0)),
        ],
    )


def routed_expert(rows, grads, w_in, w_out, place):
    senders = len(rows)
    count, operands = senders * CAP, list(rows) + list(grads)
    hidden = jax.ShapeDtypeStruct((count, w_in.shape[2]), jnp.bfloat16)
    result = ffn_call(
        lambda *refs: routed_kernel(senders, *refs),
        "routed_expert",
        operands,
        [whole(operand.shape) for operand in operands],
        w_in,
        w_out,
        place,
        [jax.ShapeDtypeStruct((CAP, D), jnp.bfloat16)] * senders
        + [jax.ShapeDtypeStruct((CAP + EXTRA, D), jnp.bfloat16)] * senders
        + [
            hidden,
            hidden,
            jax.ShapeDtypeStruct((count, D), jnp.bfloat16),
            jax.ShapeDtypeStruct((D, count), jnp.bfloat16),
        ],
        2 * senders,
        [
            pltpu.VMEM((count, D), jnp.bfloat16),
            pltpu.VMEM((count, 128), jnp.float32),
            pltpu.VMEM((count, D), jnp.float32),
            pltpu.VMEM((count, D), jnp.float32),
        ],
    )
    return (result[:senders], result[senders : 2 * senders]) + tuple(result[2 * senders :])


def expert_outer_kernel(added, which_ref, gelu_ref, grad_ref, rows_ref, pre_ref, *refs):
    out_ref, step = refs[-1], pl.program_id(0)
    chips, tall = out_ref.shape[0], gelu_ref.shape[1]
    depth, count = rows_ref.shape[2:]

    @pl.when(step < chips)
    def _():
        result = product_tn(gelu_ref[...], grad_ref[...])
        if added:
            result = result + refs[0][0].astype(jnp.float32)
        out_ref[step, :tall, :] = result.astype(jnp.bfloat16)

    @pl.when(step >= chips)
    def _():
        result = product(rows_ref[...].reshape(chips * depth, count), pre_ref[...])
        result = result.reshape(chips, depth, D)
        place = pl.ds(pl.multiple_of(tall + (step - chips) * depth, 32), depth)
        if added:
            result = result + refs[1][...].astype(jnp.float32)
        out_ref[:, place, :] = result.astype(jnp.bfloat16)


def attention_outer_kernel(added, which_ref, normed_ref, mixed_ref, projected_ref, grad_ref, *refs):
    out_ref, step = refs[-1], pl.program_id(0)
    chips = out_ref.shape[0]
    depth, count = normed_ref.shape[2:]
    place = pl.ds(pl.multiple_of(step * depth, 32), depth)

    def put(left_ref, right_ref):
        result = product(left_ref[...].reshape(chips * depth, count), right_ref[...])
        result = result.reshape(chips, depth, D)
        if added:
            result = result + refs[0][:, place, :].astype(jnp.float32)
        out_ref[:, place, :] = result.astype(jnp.bfloat16)

    @pl.when(step < 3)
    def _():
        put(normed_ref, projected_ref)

    @pl.when(step == 3)
    def _():
        put(mixed_ref, grad_ref)


def outer_call(kernel, name, steps, which, operands, specs, rows, came, came_specs, tokens, flops):
    chips = lax.axis_size("dp") // 2
    full = whole((chips, rows, D))
    extra = [] if came is None else [came] * len(came_specs or [full])
    return pl.pallas_call(
        lambda *refs: kernel(came is not None, *refs),
        grid_spec=pltpu.PrefetchScalarGridSpec(
            num_scalar_prefetch=1,
            grid=(steps,),
            in_specs=specs + (came_specs or [full])[: len(extra)] + [HBM] * len(tokens),
            out_specs=full,
        ),
        out_shape=jax.ShapeDtypeStruct((chips, rows, D), jnp.bfloat16),
        compiler_params=pltpu.CompilerParams(vmem_limit_bytes=VMEM),
        cost_estimate=pl.CostEstimate(
            flops=flops,
            bytes_accessed=sum(2 * operand.size for operand in operands) + 4 * chips * rows * D,
            transcendentals=0,
        ),
        name=name,
    )(jnp.reshape(which, (1,)).astype(jnp.int32), *operands, *extra, *tokens)


def by_device(turned):
    n_dp = lax.axis_size("dp")
    return turned.reshape(n_dp // 2, 2, turned.shape[0] // n_dp, turned.shape[1])


def plain_outer(pairs):
    n_dp = lax.axis_size("dp")

    def make(which, came, tokens):
        parts = []
        for turned, right in pairs:
            result = product(turned, right).reshape(n_dp // 2, 2, turned.shape[0] // n_dp, right.shape[1])
            result = at_place(result, which, 1).reshape(n_dp // 2, -1, right.shape[1] // D, D)
            parts.append(jnp.swapaxes(result, 1, 2).reshape(n_dp // 2, -1, D))
        parts = jnp.concatenate(parts, axis=1)
        parts = parts if came is None else parts + came.astype(jnp.float32)
        return parts.astype(jnp.bfloat16)

    return make


def expert_outer(gelu, grad, turned, grad_pre):
    n_dp, (count, ff) = lax.axis_size("dp"), gelu.shape
    chips, tall, depth = n_dp // 2, ff // n_dp, D // n_dp
    if tall % 128 or depth % 32:
        return plain_outer([(jnp.swapaxes(gelu, 0, 1), grad), (turned, grad_pre)])
    turned = by_device(turned)
    specs = [
        pl.BlockSpec((count, tall), lambda i, which: (0, 2 * jnp.minimum(i, chips - 1) + which[0])),
        whole((count, D)),
        pl.BlockSpec((chips, 1, depth, count), lambda i, which: (0, which[0], 0, 0)),
        pl.BlockSpec((count, D), lambda i, which: (0, jnp.maximum(i - chips, 0))),
    ]
    return lambda which, came, tokens: outer_call(
        expert_outer_kernel,
        "expert_outer",
        chips + ff // D,
        which,
        [gelu, grad, turned, grad_pre],
        specs,
        tall + ff // D * depth,
        came,
        [
            pl.BlockSpec((1, tall, D), lambda i, which: (jnp.minimum(i, chips - 1), 0, 0)),
            pl.BlockSpec(
                (chips, depth, D), lambda i, which: (0, tall // depth + jnp.maximum(i - chips, 0), 0)
            ),
        ],
        tokens,
        2 * count * D * ff,
    )


def attention_outer(left, grad_projected, grad_att):
    n_dp = lax.axis_size("dp")
    chips, depth = n_dp // 2, D // n_dp
    if depth % 32:
        return plain_outer([(left[0], grad_projected), (left[1], grad_att)])
    own = pl.BlockSpec((chips, 1, depth, LONG), lambda i, which: (0, which[0], 0, 0))
    specs = [
        own,
        own,
        pl.BlockSpec((LONG, D), lambda i, which: (0, jnp.minimum(i, 2))),
        whole((LONG, D)),
    ]
    operands = [by_device(left[0]), by_device(left[1]), grad_projected, grad_att]
    return lambda which, came, tokens: outer_call(
        attention_outer_kernel,
        "attention_outer",
        4,
        which,
        operands,
        specs,
        4 * depth,
        came,
        None,
        tokens,
        4 * LONG * D * D,
    )


def to_core(make, tokens=()):
    return make(1 - lax.axis_index("dp") % 2, None, list(tokens))


def from_core(sent):
    return lax.ppermute(sent, "dp", [(i, i ^ 1) for i in range(lax.axis_size("dp"))])


def with_core(make, came, tokens=()):
    return make(lax.axis_index("dp") % 2, came, list(tokens))


def combine_kernel(count, dotted, ids_ref, slots_ref, base_ref, *refs):
    block_refs, refs = refs[:count], refs[count:]
    out_ref, dots_out_ref, rows_ref, dots_ref = refs
    size = block_refs[0].shape[0]

    @pl.when(pl.program_id(0) == 0)
    def _():
        for at, block_ref in enumerate(block_refs):
            rows_ref[at * size : (at + 1) * size, :] = block_ref[...]
            if dotted:
                pieces = block_ref[CAP:, :size].astype(jnp.float32)
                dots_ref[:, at * size : (at + 1) * size] = pieces[0:1] + pieces[1:2] + pieces[2:3]

    ids = ids_ref[...]
    first, second = slots_ref[:, 0:1] == ids, slots_ref[:, 1:2] == ids
    hold = jnp.where(first | second, 1.0, 0.0).astype(jnp.bfloat16)
    out_ref[...] = base_ref[...] + product(hold, rows_ref[...])
    if dotted:
        dots = dots_ref[...]
        dots_out_ref[:, 0:1] = jnp.sum(jnp.where(first, dots, 0.0), axis=1, keepdims=True)
        dots_out_ref[:, 1:2] = jnp.sum(jnp.where(second, dots, 0.0), axis=1, keepdims=True)


def combine(ids, slots, base, blocks, dotted):
    total = ids.shape[1]
    patch = pl.BlockSpec((SHORT, D), lambda i: (i, 0))
    pair = pl.BlockSpec((SHORT, 2), lambda i: (i, 0))
    return pl.pallas_call(
        lambda *refs: combine_kernel(len(blocks), dotted, *refs),
        grid=(BLOCKS,),
        in_specs=[whole(ids.shape), pair, patch] + [whole(block.shape) for block in blocks],
        out_specs=[patch, pair],
        out_shape=[
            jax.ShapeDtypeStruct((LONG, D), jnp.float32),
            jax.ShapeDtypeStruct((LONG, 2), jnp.float32),
        ],
        scratch_shapes=[pltpu.VMEM((total, D), jnp.bfloat16), pltpu.VMEM((1, total), jnp.float32)],
        compiler_params=pltpu.CompilerParams(vmem_limit_bytes=VMEM),
        cost_estimate=pl.CostEstimate(
            flops=2 * LONG * total * D, bytes_accessed=2 * total * D + 8 * LONG * D, transcendentals=0
        ),
        name="combine",
    )(ids, slots, base, *blocks)


def sums_kernel(groups, *refs):
    out_ref, in_ref = refs[-2:]
    depth, wide = in_ref.shape[1:]
    expert, step = pl.program_id(0), pl.program_id(1)
    start = 0
    for at, count in enumerate(groups):
        parts = refs[start : start + count]
        start += count

        @pl.when(expert == at)
        def _(parts=parts):
            total = parts[0][...].astype(jnp.float32)
            for part in parts[1:]:
                total = total + part[...].astype(jnp.float32)

            @pl.when(step == 0)
            def _():
                out_ref[0] = total

            @pl.when(step == 1)
            def _():
                for j in range(wide // D):
                    in_ref[0, :, j * D : (j + 1) * D] = total[j * depth : (j + 1) * depth, :]


def expert_sums(pieces, tall, depth, wide):
    count = len(pieces)

    def spec(at, row):
        def index(expert, step):
            return row // tall + jnp.where(expert == at, step, 0 if at else 1), 0

        return pl.BlockSpec((tall, D), index)

    return pl.pallas_call(
        lambda *refs: sums_kernel([len(group) for group in pieces], *refs),
        grid=(count, 2),
        in_specs=[spec(at, row) for at, group in enumerate(pieces) for _, row in group],
        out_specs=[
            pl.BlockSpec((1, tall, D), lambda expert, step: (expert, 0, 0)),
            pl.BlockSpec((1, depth, wide), lambda expert, step: (expert, 0, 0)),
        ],
        out_shape=[
            jax.ShapeDtypeStruct((count, tall, D), jnp.float32),
            jax.ShapeDtypeStruct((count, depth, wide), jnp.float32),
        ],
        compiler_params=pltpu.CompilerParams(vmem_limit_bytes=VMEM),
        cost_estimate=pl.CostEstimate(
            flops=0, bytes_accessed=32 * count * tall * D, transcendentals=0
        ),
        name="expert_sums",
    )(*[array for group in pieces for array, _ in group])


def dispatch_kernel(count, ids_ref, slots_ref, gates_ref, rows_ref, *out_refs):
    size = ids_ref.shape[0] // count
    for at, out_ref in enumerate(out_refs):
        ids = ids_ref[at * size : (at + 1) * size, :]
        first, second = slots_ref[0:1, :] == ids, slots_ref[1:2, :] == ids
        hold = jnp.where(first | second, 1.0, 0.0).astype(jnp.bfloat16)
        out_ref[:CAP, :] = product(hold, rows_ref[...])[:CAP].astype(jnp.bfloat16)
        gates = jnp.where(first, gates_ref[0:1, :], 0.0) + jnp.where(second, gates_ref[1:2, :], 0.0)
        out_ref[CAP:, :] = below(jnp.sum(gates, axis=1, keepdims=True)[:CAP])


def dispatch(ids, slots, gates, rows, count):
    size = ids.shape[0] // count
    return pl.pallas_call(
        lambda *refs: dispatch_kernel(count, *refs),
        out_shape=[jax.ShapeDtypeStruct((size, D), jnp.bfloat16)] * count,
        compiler_params=pltpu.CompilerParams(vmem_limit_bytes=VMEM),
        cost_estimate=pl.CostEstimate(
            flops=2 * LONG * ids.shape[0] * D, bytes_accessed=2 * (LONG + ids.shape[0]) * D, transcendentals=0
        ),
        name="dispatch",
    )(ids, slots, gates, rows)


def gather_kernel(n_dp, n_ex, own_ref, all_ref, here_sem, z_out, z_in, chip_out, chip_in, core_out, core_in):
    dp, ex = lax.axis_index("dp"), lax.axis_index("expert")
    chips = n_dp // 2

    def along(axis, distance):
        if axis == "expert":
            return (dp, ex ^ distance)
        return (dp ^ distance, ex)

    routes = (
        [("expert", k) for k in range(1, n_ex)] + [("dp", 2 * k) for k in range(1, chips)] + [("dp", 1)]
    )
    barrier = pltpu.get_barrier_semaphore()
    for route in routes:
        pl.semaphore_signal(barrier, inc=1, device_id=along(*route), device_id_type=pl.DeviceIdType.MESH)
    pl.semaphore_wait(barrier, len(routes))

    def send(source, target, sent, came, device):
        copy = pltpu.make_async_remote_copy(
            src_ref=source,
            dst_ref=target,
            send_sem=sent,
            recv_sem=came,
            device_id=device,
            device_id_type=pl.DeviceIdType.MESH,
        )
        copy.start()
        return copy

    def wait_for(target, came):
        pltpu.make_async_remote_copy(
            src_ref=target,
            dst_ref=target,
            send_sem=came,
            recv_sem=came,
            device_id=(dp, ex),
            device_id_type=pl.DeviceIdType.MESH,
        ).wait_recv()

    def group(device, first=0, count=n_ex):
        return all_ref.at[pl.ds(device * n_ex + first, count)]

    mine = all_ref.at[dp * n_ex + ex]
    here = pltpu.make_async_copy(own_ref, mine, here_sem)
    here.start()
    sends = [
        send(own_ref, mine, z_out.at[k], z_in.at[k], along("expert", k)) for k in range(1, n_ex)
    ]
    for k in range(1, n_ex):
        wait_for(all_ref.at[dp * n_ex + (ex ^ k)], z_in.at[k])
    here.wait()
    direct = [1, 2] if chips == 4 else list(range(1, chips))
    for k in direct:
        sends.append(send(group(dp), group(dp), chip_out.at[k], chip_in.at[k], along("dp", 2 * k)))
    sends.append(send(group(dp), group(dp), core_out.at[0], core_in.at[0], along("dp", 1)))
    for k in direct:
        other = dp ^ (2 * k)
        wait_for(group(other), chip_in.at[k])
        if chips == 4:
            part = group(other, (k - 1) * (n_ex // 2), n_ex // 2)
            sends.append(send(part, part, chip_out.at[2 + k], chip_in.at[2 + k], along("dp", 2 * (3 - k))))
        sends.append(send(group(other), group(other), core_out.at[k], core_in.at[k], along("dp", 1)))
    if chips == 4:
        other = dp ^ 6
        for k in direct:
            wait_for(group(other, (k - 1) * (n_ex // 2), n_ex // 2), chip_in.at[2 + k])
        sends.append(send(group(other), group(other), core_out.at[3], core_in.at[3], along("dp", 1)))
    for k in range(chips):
        wait_for(group(dp ^ (2 * k) ^ 1), core_in.at[k])
    for copy in sends:
        copy.wait_send()


def gather(own):
    n_dp, n_ex = lax.axis_size("dp"), lax.axis_size("expert")
    chips = n_dp // 2
    counts = (n_ex, n_ex, max(chips, 5), max(chips, 5), chips, chips)
    return pl.pallas_call(
        lambda *refs: gather_kernel(n_dp, n_ex, *refs),
        in_specs=[HBM],
        out_specs=HBM,
        out_shape=jax.ShapeDtypeStruct((n_dp * n_ex,) + own.shape, own.dtype),
        scratch_shapes=[pltpu.SemaphoreType.DMA] + [pltpu.SemaphoreType.DMA((count,)) for count in counts],
        compiler_params=pltpu.CompilerParams(collective_id=0, has_side_effects=True),
        cost_estimate=pl.CostEstimate(flops=0, bytes_accessed=64 * own.size, transcendentals=0),
        name="gather",
    )(own)


def swap(parts, axis):
    return lax.all_to_all(parts, axis, 0, 0, tiled=True)


def at_place(parts, place, axis=0):
    return lax.dynamic_index_in_dim(parts, place, axis, keepdims=False)


def from_expert(parts):
    size, me = parts.shape[0], lax.axis_index("expert")
    arrived = [at_place(parts, me)]
    for distance in range(1, size):
        route = [(i, i ^ distance) for i in range(size)]
        arrived.append(lax.ppermute(at_place(parts, me ^ distance), "expert", route))
    return arrived


def together(live, work, *operands):
    def never(*operands):
        return jax.tree.map(lambda out: jnp.zeros(out.shape, out.dtype), jax.eval_shape(work, *operands))

    return lax.cond(live, work, never, *operands)


def to_expert(blocks, distances=None):
    size = len(blocks)
    return [
        lax.ppermute(blocks[distance], "expert", [(i, i ^ distance) for i in range(size)])
        if distance
        else blocks[0]
        for distance in (range(size) if distances is None else distances)
    ]


def from_chips(parts, distances):
    chips, me = lax.axis_size("dp") // 2, lax.axis_index("dp") // 2
    arrived = []
    for distance in distances if parts else []:
        route = [(i, i ^ (2 * distance)) for i in range(2 * chips)]
        part = jnp.concatenate([at_place(array, me ^ distance) for array in parts], axis=0)
        arrived.append(lax.ppermute(part, "dp", route) if distance else part)
    return arrived


def total_of(arrived):
    total = arrived[0].astype(jnp.float32)
    for part in arrived[1:]:
        total = total + part.astype(jnp.float32)
    return total


def body(
    tokens,
    bucket,
    image_length,
    routes,
    cotangent,
    w_qkv,
    w_out,
    w_ada,
    b_ada,
    w_router,
    w_shared_in,
    w_shared_out,
    w_expert_in,
    w_expert_out,
):
    n_dp, n_ex = lax.axis_size("dp"), lax.axis_size("expert")
    n, chips = n_dp * n_ex, n_dp // 2
    dp = lax.axis_index("dp")
    share = D // n
    ff = w_shared_in.shape[1]
    wide = w_ada.shape[1]
    column = wide // n

    ada_parts = jnp.swapaxes(w_ada.reshape(share, n, column), 0, 1)
    bucket_row = jnp.zeros((1, 1, column), jnp.bfloat16).at[0, 0, :BLOCKS].set(bucket.astype(jnp.bfloat16))
    ada_parts = jnp.concatenate([ada_parts, jnp.broadcast_to(bucket_row, (n, 1, column))], axis=1)
    ada_parts = swap(ada_parts, BOTH)
    ada_columns = ada_parts[:, :share].reshape(D, column)
    buckets = ada_parts[:, share, :BLOCKS].astype(jnp.int32).reshape(n * BLOCKS)
    condition = jax.nn.silu(embed(buckets)).astype(jnp.bfloat16)
    modulation = product(condition, ada_columns) + b_ada.astype(jnp.float32)
    w_qkv = w_qkv + (0.0 * modulation[0, 0]).astype(jnp.bfloat16)
    modulation = swap(modulation.reshape(n, BLOCKS, column), BOTH)
    modulation = jnp.swapaxes(modulation, 0, 1).reshape(BLOCKS, wide)

    def span(index):
        return expand(modulation[:, index * D : (index + 1) * D])

    shift_one, scale_one, gate_one, shift_two, scale_two, gate_two = [span(index) for index in range(6)]

    w_qkv = gather(w_qkv).reshape(D, 3 * D)
    router_rows = jnp.zeros((8, D), jnp.bfloat16).at[0, : share * EXPERTS].set(w_router.reshape(-1))
    packed = jnp.concatenate(
        [w_shared_out, w_out]
        + [w_shared_in[:, at * D : (at + 1) * D] for at in range(ff // D)]
        + [router_rows],
        axis=0,
    )
    packed = lax.all_gather(packed, BOTH, axis=0, tiled=False)
    start = ff // n
    w_out = packed[:, start : start + share].reshape(D, D)
    w_shared_in = packed[:, start + share : start + (1 + ff // D) * share].reshape(n, ff // D, share, D)
    w_shared_in = jnp.swapaxes(w_shared_in, 0, 1).reshape(ff // D, D, D)
    w_router = packed[:, start + (1 + ff // D) * share, : share * EXPERTS].reshape(D, EXPERTS)
    if start % 16 == 0:
        w_shared_out = packed, pl.BlockSpec((D // start, start, D), lambda step: (step, 0, 0))
    else:
        w_shared_out = packed[:, :start].reshape(1, ff, D), None

    choose = [routes[:, k : k + 1] == jnp.arange(EXPERTS, dtype=jnp.int32)[None, :] for k in range(2)]
    named = (choose[0] | choose[1]).astype(jnp.bfloat16)
    position = jnp.arange(LONG, dtype=jnp.int32)
    earlier = (position[:, None] > position[None, :]).astype(jnp.bfloat16)
    before = product(earlier, named)
    slots = [
        routes[:, k] * CAP + jnp.sum(jnp.where(choose[k], before, 0.0), axis=1).astype(jnp.int32)
        for k in range(2)
    ]
    local = EXPERTS // n_ex
    ex = lax.axis_index("expert")
    near = jnp.stack([ex ^ k for k in range(n_ex)]).astype(jnp.int32)

    def slot_ids(which, size):
        place = jnp.arange(size, dtype=jnp.int32)
        experts = jnp.asarray(which, jnp.int32)[:, None] + near[None, :] * local
        return jnp.where(place < CAP, (experts * CAP)[:, :, None] + place, -1).reshape(-1)

    def hold(at, size):
        ids = slot_ids([at], size)[:, None]
        return ((ids == slots[0][None, :]) | (ids == slots[1][None, :])).astype(jnp.bfloat16)

    slot_pairs = jnp.stack(slots, axis=1)

    grad_out = cotangent.astype(jnp.float32)
    grad_mlp = (gate_two * grad_out).astype(jnp.bfloat16)

    def grad_blocks(at, grad_mlp):
        blocks = product(hold(at, CAP), grad_mlp).astype(jnp.bfloat16).reshape(n_ex, CAP, D)
        return [blocks[k] for k in range(n_ex)]

    grad_sent = grad_blocks(0, grad_mlp)
    live = image_length[0] > 0

    inputs_full = tokens.astype(jnp.float32)
    hat_one, inverse_one = normalize(inputs_full)
    normed_one = (hat_one * (1.0 + scale_one) + shift_one).astype(jnp.bfloat16)
    projected = product(normed_one, w_qkv).astype(jnp.bfloat16)
    def attention_part(projected, blocks, grad_mlp):
        others = [grad_blocks(at, grad_mlp) for at in range(1, local)]
        return *attend(image_length, projected), to_expert(blocks), others

    attended, log_total, grad_rows, grad_sent = together(
        live, attention_part, projected, grad_sent, grad_mlp
    )
    grad_rows = [grad_rows]
    branch_att = product(attended, w_out)
    hidden_one = inputs_full + gate_one * branch_att
    hat_two, inverse_two = normalize(hidden_one)
    normed_two = (hat_two * (1.0 + scale_two) + shift_two).astype(jnp.bfloat16)

    logits = product(normed_two, w_router)
    picked_logits = jnp.stack([jnp.sum(jnp.where(pick, logits, 0.0), axis=-1) for pick in choose], axis=-1)
    gate_weights = jax.nn.softmax(picked_logits, axis=-1)
    full = CAP + EXTRA

    blocks = dispatch(
        slot_ids(range(local), full)[:, None],
        jnp.stack(slots),
        jnp.swapaxes(gate_weights, 0, 1),
        normed_two,
        local * n_ex,
    )
    sent = [blocks[at * n_ex : (at + 1) * n_ex] for at in range(local)]

    tall = ff // n_dp
    size = tall + ff // D * (D // n_dp)
    near_chips, far_chips = list(range(min(3, chips))), list(range(3, chips))

    def split_expert(part):
        blocks = jnp.swapaxes(part[tall:].reshape(ff // D, D // n_dp, D), 0, 1)
        return part[:tall], blocks.reshape(D // n_dp, ff)

    pieces = [[] for _ in range(1 + local)]

    def note(arrays, *which):
        for row, at in enumerate(which):
            pieces[at] += [(array, row * size) for array in arrays]

    def sum_of(at):
        return total_of([array[row : row + size] for array, row in pieces[at]])

    def first_part(normed_two, grad_mlp, blocks):
        results = shared_expert(normed_two, grad_mlp, w_shared_in, w_shared_out)
        half = to_core(expert_outer(results[2], grad_mlp, results[4], results[3]))
        return results, half, to_expert(blocks)

    results, shared_half, arrived = together(live, first_part, normed_two, grad_mlp, sent[0])
    shared, grad_normed_two, gelu_shared, grad_pre_shared, turned_shared = results

    def second_part(rows, grads, others):
        results = routed_expert(rows, grads, w_expert_in, w_expert_out, 0)
        half = to_core(expert_outer(results[2], results[4], results[5], results[3]))
        return results, half, [to_expert(blocks) for blocks in others]

    def weights_part(gelu, weighted, turned, grad_pre, half, shared_half, grads):
        came = [from_core(half), from_core(shared_half)]
        kept = [with_core(expert_outer(gelu, weighted, turned, grad_pre), came[0])]
        make = expert_outer(gelu_shared, grad_mlp, turned_shared, grad_pre_shared)
        kept.append(with_core(make, came[1], kept))
        return kept, [to_expert(blocks) for blocks in grads]

    results, half, others = together(live, second_part, arrived, grad_rows[0], sent[1:])
    outs, backs, gelu, grad_pre, weighted, turned_rows = results
    arrived = [arrived] + others
    (kept_first, kept_shared), others = together(
        live, weights_part, gelu, weighted, turned_rows, grad_pre, half, shared_half, grad_sent
    )
    grad_rows += others
    out_rows, grad_home, kept_last = [outs], [], []

    def third_part(rows, grads, at, backs, kept):
        results = routed_expert(rows, grads, w_expert_in, w_expert_out, at)
        half = to_core(expert_outer(results[2], results[4], results[5], results[3]))
        return results, half, to_expert(backs), from_chips(kept, near_chips)

    def fourth_part(gelu, weighted, turned, grad_pre, half, backs, kept):
        kept_now = with_core(expert_outer(gelu, weighted, turned, grad_pre), from_core(half))
        return kept_now, to_expert(backs), from_chips(kept, far_chips), [turn(normed_one), turn(attended)]

    if local == 1:
        turned = [turn(normed_one), turn(attended)]
        backs = to_expert(backs)
        note(from_chips([kept_first], near_chips), 0)
        note(from_chips([kept_shared], near_chips + far_chips), 1)
    for at in range(1, local):
        results, half, home, part = together(
            live,
            lambda rows, grads, backs, kept, at=at: third_part(rows, grads, at, backs, kept),
            arrived[at],
            grad_rows[at],
            backs,
            [kept_first, kept_shared] if at == 1 else kept_last[-1:],
        )
        note(part, *((0, 1) if at == 1 else (at,)))
        outs, backs, gelu, grad_pre, weighted, turned_rows = results
        out_rows.append(outs)
        grad_home.append(home)
        kept_now, backs, part, turned = together(
            live,
            fourth_part,
            gelu,
            weighted,
            turned_rows,
            grad_pre,
            half,
            backs,
            [kept_shared] if at == 1 else kept_last[-1:],
        )
        note(part, 1 if at == 1 else at)
        kept_last.append(kept_now)
    grad_home.append(backs)

    def fifth_part(grad_normed_two, grad_home, others, kept):
        ids = slot_ids(range(local), full)[None, :]
        grad_normed_two, grad_gates = combine(ids, slot_pairs, grad_normed_two, sum(grad_home, []), True)
        grad_picked = gate_weights * (
            grad_gates - jnp.sum(gate_weights * grad_gates, axis=1, keepdims=True)
        )
        grad_logits = jnp.where(choose[0], grad_picked[:, 0:1], 0.0) + jnp.where(
            choose[1], grad_picked[:, 1:2], 0.0
        )
        logit_parts = jnp.concatenate(split_three(grad_logits), axis=1).astype(jnp.bfloat16)
        grad_router = product_tn(normed_two, logit_parts).reshape(D, 3, EXPERTS).sum(axis=1)
        grad_normed_two = grad_normed_two + product_nt(
            logit_parts, jnp.concatenate([w_router, w_router, w_router], axis=1)
        )

        grad_hidden_one = cotangent.astype(jnp.float32) + norm_back(
            grad_normed_two * (1.0 + span(4)), hat_two, inverse_two
        )
        grad_att = (span(2) * grad_hidden_one).astype(jnp.bfloat16)
        grad_attended = product_nt(grad_att, w_out).astype(jnp.bfloat16)
        grad_spans = [
            block_sums(grad_hidden_one * product(attended, w_out)),
            block_sums(grad_normed_two),
            block_sums(grad_normed_two * hat_two),
        ]
        results = (grad_router, grad_spans, grad_hidden_one, grad_att, grad_attended)
        return results, [to_expert(blocks) for blocks in others], from_chips(kept, near_chips)

    results, returned, part = together(
        live, fifth_part, grad_normed_two, grad_home, out_rows[:-1], kept_last[-1:]
    )
    grad_router, grad_spans, grad_hidden_one, grad_att, grad_attended = results
    note(part, local)

    def sixth_part(projected, grad_attended, attended, log_total, blocks, kept):
        result = attend_back(image_length, projected, grad_attended, attended, log_total)
        half = to_core(attention_outer(turned, result, grad_att))
        grad_shared_out, grad_shared_in = split_expert(sum_of(1).astype(jnp.bfloat16))
        rows = (D // n_dp) * (ff // n_ex) // D
        shared_parts = jnp.concatenate(
            [
                jnp.swapaxes(grad_shared_in.reshape(D // n_dp, n_ex, ff // n_ex), 0, 1).reshape(
                    n_ex, rows, D
                ),
                jnp.swapaxes(grad_shared_out.reshape(ff // n_dp, n_ex, D // n_ex), 0, 1).reshape(
                    n_ex, rows, D
                ),
            ],
            axis=1,
        )
        return result, half, to_expert(blocks), from_chips(kept, far_chips), shared_parts

    grad_projected, half, rows, part, shared_parts = together(
        live,
        sixth_part,
        projected,
        grad_attended,
        attended,
        log_total,
        out_rows[-1],
        [kept_first] + kept_last[-1:],
    )
    note(part, *([0, local] if local > 1 else [0]))
    returned.append(rows)

    def seventh_part(grad_projected, half, shared_parts):
        came = from_core(half)
        grad_normed_one = product_nt(grad_projected, w_qkv)
        hat_one, inverse_one = normalize(tokens.astype(jnp.float32))
        grad_input = grad_hidden_one + norm_back(
            grad_normed_one * (1.0 + span(1)), hat_one, inverse_one
        )
        spans = [block_sums(grad_normed_one), block_sums(grad_normed_one * hat_one)]
        kept = with_core(attention_outer(turned, grad_projected, grad_att), came)
        return grad_input.astype(jnp.bfloat16), spans, kept, from_expert(shared_parts)

    grad_input, spans, kept, shared_parts = together(
        live, seventh_part, grad_projected, half, shared_parts
    )

    def eighth_part(kept, returned):
        arrived = from_chips([kept], list(range(chips)))
        routed = [group for at, group in enumerate(pieces) if at != 1]
        grad_expert_out, grad_expert_in = expert_sums(routed, tall, D // n_dp, ff)
        ids = slot_ids(range(local), CAP)[None, :]
        branch_mlp = combine(ids, slot_pairs, shared, sum(returned, []), False)[0]
        result = hidden_one + span(5) * branch_mlp
        last_span = block_sums(cotangent.astype(jnp.float32) * branch_mlp)
        return arrived, grad_expert_out, grad_expert_in, result.astype(jnp.bfloat16), last_span

    attention_parts, grad_expert_out, grad_expert_in, result, last_span = together(
        live, eighth_part, kept, returned
    )
    grad_modulation = jnp.concatenate(spans + grad_spans + [last_span], axis=1)

    own_wide, router_rows, router_columns = wide // n_ex, D // n_dp, EXPERTS // n_ex
    by_expert = jnp.swapaxes(grad_modulation.reshape(BLOCKS, n_ex, own_wide), 0, 1)
    message = jnp.concatenate(
        [
            jnp.broadcast_to(
                by_expert.reshape(1, n_ex, BLOCKS * own_wide), (n_dp, n_ex, BLOCKS * own_wide)
            ),
            jnp.sum(grad_modulation, axis=0).reshape(n_dp, n_ex, column),
            jnp.swapaxes(grad_router.reshape(n_dp, router_rows, n_ex, router_columns), 1, 2).reshape(
                n_dp, n_ex, router_rows * router_columns
            ),
        ],
        axis=2,
    )
    length = message.shape[2]
    message = jnp.pad(message.astype(jnp.bfloat16), ((0, 0), (0, 0), (0, -length % 128))).reshape(n, -1, 128)
    message = swap(message, BOTH).reshape(n, -1).astype(jnp.float32)
    at = BLOCKS * own_wide
    every_modulation = message[:, :at].reshape(n * BLOCKS, own_wide)
    grad_b_ada = jnp.sum(message[:, at : at + column], axis=0)
    grad_router = jnp.sum(message[:, at + column : length], axis=0).reshape(router_rows, router_columns)
    own_condition = lax.dynamic_slice_in_dim(condition, dp * (D // n_dp), D // n_dp, axis=1)

    attention_parts = total_of(attention_parts).astype(jnp.bfloat16).reshape(4, D // n_dp, D)
    attention_parts = jnp.concatenate(
        [
            jnp.swapaxes(attention_parts[:3], 0, 1).reshape(D // n_dp, n_ex, 3 * D // n_ex),
            attention_parts[3].reshape(D // n_dp, n_ex, D // n_ex),
        ],
        axis=2,
    )
    rest = (D // n_dp) * 4 // n_ex
    attention_parts = jnp.swapaxes(attention_parts, 0, 1).reshape(n_ex, rest, D)

    parts = together(live, from_expert, attention_parts)
    grad_w_ada = lax.dot_general(
        own_condition.astype(jnp.float32),
        every_modulation,
        (((0,), (0,)), ((), ())),
        precision=HIGHEST,
        preferred_element_type=jnp.float32,
    )
    attention_parts = total_of(parts).reshape(D // n_dp, 4 * D // n_ex)
    shared_parts = total_of(shared_parts)
    half = shared_parts.shape[0] // 2
    return (
        result,
        grad_input,
        attention_parts[:, : 3 * D // n_ex],
        attention_parts[:, 3 * D // n_ex :],
        grad_w_ada,
        grad_b_ada,
        grad_router,
        shared_parts[:half].reshape(D // n_dp, ff // n_ex),
        shared_parts[half:].reshape(ff // n_dp, D // n_ex),
        grad_expert_in,
        grad_expert_out,
    )


def solution(mesh):
    rows, flat = P(BOTH, None), P(BOTH)
    spread = P("dp", "expert")
    return jax.shard_map(
        body,
        mesh=mesh,
        in_specs=(
            rows,
            flat,
            flat,
            rows,
            rows,
            rows,
            rows,
            rows,
            flat,
            rows,
            rows,
            rows,
            P("expert", None, None),
            P("expert", None, None),
        ),
        out_specs=(
            rows,
            rows,
            spread,
            spread,
            spread,
            flat,
            spread,
            spread,
            spread,
            P("expert", "dp", None),
            P("expert", "dp", None),
        ),
        check_vma=False,
    )
```

```python
import math

import jax
import jax.numpy as jnp
from jax import lax
from jax.experimental import pallas as pl
from jax.experimental.pallas import tpu as pltpu
from jax.sharding import PartitionSpec as P

D = 768
HEADS = 12
HEAD_DIM = 64
EXPERTS = 8
LONG = 1024
SHORT = 256
BLOCKS = LONG // SHORT
CAP = 288
EXTRA = 16
BUCKETS = 50
PAIRS = HEADS // 2
FAR = 1e30
VMEM = 60 * 2**20

HIGHEST = lax.Precision.HIGHEST
BOTH = ("dp", "expert")
HBM = pl.BlockSpec(memory_space=pl.ANY)


def product(left_side, right_side):
    return jnp.dot(left_side, right_side, preferred_element_type=jnp.float32)


def product_nt(left_side, right_side):
    return lax.dot_general(
        left_side, right_side, (((1,), (1,)), ((), ())), preferred_element_type=jnp.float32
    )


def product_tn(left_side, right_side):
    return lax.dot_general(
        left_side, right_side, (((0,), (0,)), ((), ())), preferred_element_type=jnp.float32
    )


def embed(bucket):
    time_values = bucket.astype(jnp.float32) * (1000.0 / BUCKETS)
    half_width = D // 2
    frequency = jnp.exp(-math.log(10000.0) * jnp.arange(half_width, dtype=jnp.float32) / half_width)
    angles = time_values[:, None] * frequency[None, :]
    return jnp.concatenate([jnp.cos(angles), jnp.sin(angles)], axis=1)


def normalize(values):
    center = values - jnp.mean(values, axis=-1, keepdims=True)
    variance = jnp.mean(center * center, axis=-1, keepdims=True)
    inverse = lax.rsqrt(variance + 1e-06)
    return (center * inverse, inverse)


def norm_back(grad_hat, hat_values, inverse):
    return inverse * (
        grad_hat
        - jnp.mean(grad_hat, axis=-1, keepdims=True)
        - hat_values * jnp.mean(grad_hat * hat_values, axis=-1, keepdims=True)
    )


def expand(block_rows):
    return jnp.repeat(block_rows, SHORT, axis=0)


def block_sums(values):
    return jnp.sum(values.reshape(BLOCKS, SHORT, D), axis=1)


def split_three(values):
    first = lax.reduce_precision(values, 8, 7)
    second = lax.reduce_precision(values - first, 8, 7)
    return first, second, values - first - second


def attend_kernel(length_ref, q_ref, k_ref, v_ref, out_ref, total_ref):
    far = jnp.where(length_ref[0] == LONG, 0.0, FAR)
    lane = lax.broadcasted_iota(jnp.int32, (1, 2 * HEAD_DIM), 1)
    first = lane < HEAD_DIM
    keys, vals = k_ref[...], v_ref[...]
    zero, one = jnp.zeros_like(keys), jnp.ones_like(vals)
    key_set = (jnp.where(first, keys, zero), jnp.where(first, zero, keys))
    value_set = (jnp.where(first, vals, one), jnp.where(first, one, vals))
    for i in range(BLOCKS):
        rows = slice(i * SHORT, (i + 1) * SHORT)
        q = q_ref[rows, :] * jnp.asarray(HEAD_DIM**-0.5, jnp.bfloat16)
        outs, totals = [], []
        for h in range(2):
            scores = product_nt(q, key_set[h])
            parts = [scores[:, j * SHORT : (j + 1) * SHORT] for j in range(BLOCKS)]
            away = [0.0 if i == j else far for j in range(BLOCKS)]
            peak = None
            for part, distance in zip(parts, away):
                here = jnp.max(part, axis=1, keepdims=True) - distance
                peak = here if peak is None else jnp.maximum(peak, here)
            soft = jnp.concatenate(
                [
                    jnp.exp(part - (peak + distance)).astype(jnp.bfloat16)
                    for part, distance in zip(parts, away)
                ],
                axis=1,
            )
            mixed = product(soft, value_set[h])
            total = mixed[:, HEAD_DIM : HEAD_DIM + 1] if h == 0 else mixed[:, 0:1]
            outs.append(mixed / total)
            totals.append(peak + jnp.log(total))
        out_ref[rows, :] = jnp.where(first, outs[0], outs[1]).astype(jnp.bfloat16)
        flipped = jnp.transpose(jnp.where(first, totals[0], totals[1]))
        total_ref[0, 0:1, rows] = flipped[0:1, :]
        total_ref[0, 1:2, rows] = flipped[HEAD_DIM : HEAD_DIM + 1, :]


def attend_back_kernel(
    length_ref, q_ref, k_ref, v_ref, grad_ref, out_ref, total_ref, result_ref, sum_ref
):
    pair = pl.program_id(0)
    far = jnp.where(length_ref[0] == LONG, 0.0, FAR)
    lane = lax.broadcasted_iota(jnp.int32, (1, 2 * HEAD_DIM), 1)
    first = lane < HEAD_DIM
    place = lax.broadcasted_iota(jnp.int32, (1, LONG), 1) // SHORT
    q = q_ref[...] * jnp.asarray(HEAD_DIM**-0.5, jnp.bfloat16)
    grad, keys = grad_ref[...], k_ref[...]
    zero = jnp.zeros_like(keys)
    query_set = (jnp.where(first, q, zero), jnp.where(first, zero, q))
    grad_set = (jnp.where(first, grad, zero), jnp.where(first, zero, grad))
    key_set = (jnp.where(first, keys, zero), jnp.where(first, zero, keys))
    flipped = jnp.transpose(grad.astype(jnp.float32) * out_ref[...].astype(jnp.float32))
    deltas = (
        jnp.sum(flipped[:HEAD_DIM], axis=0, keepdims=True),
        jnp.sum(flipped[HEAD_DIM:], axis=0, keepdims=True),
    )
    lanes = pl.ds(pl.multiple_of(pair * 2 * HEAD_DIM, 2 * HEAD_DIM), 2 * HEAD_DIM)
    lanes_k = pl.ds(pl.multiple_of(D + pair * 2 * HEAD_DIM, 2 * HEAD_DIM), 2 * HEAD_DIM)
    lanes_v = pl.ds(pl.multiple_of(2 * D + pair * 2 * HEAD_DIM, 2 * HEAD_DIM), 2 * HEAD_DIM)
    for j in range(BLOCKS):
        rows = slice(j * SHORT, (j + 1) * SHORT)
        key_rows, value_rows = k_ref[rows, :], v_ref[rows, :]
        grad_keys = grad_values = 0.0
        for h in range(2):
            total = total_ref[0, h : h + 1, :] + jnp.where(place == j, 0.0, far)
            soft = jnp.exp(product_nt(key_rows, query_set[h]) - total)
            grad_soft = product_nt(value_rows, grad_set[h])
            grad_scores = (soft * (grad_soft - deltas[h])).astype(jnp.bfloat16)
            grad_values += product(soft.astype(jnp.bfloat16), grad_set[h])
            grad_keys += product(grad_scores, query_set[h])
            update = product_tn(grad_scores, key_set[h][rows, :])
            if j == 0 and h == 0:
                sum_ref[...] = update
            else:
                sum_ref[...] += update
        result_ref[rows, lanes_k] = grad_keys.astype(jnp.bfloat16)
        result_ref[rows, lanes_v] = grad_values.astype(jnp.bfloat16)
    result_ref[:, lanes] = (sum_ref[...] * HEAD_DIM**-0.5).astype(jnp.bfloat16)


def column_spec(start):
    return pl.BlockSpec((LONG, 2 * HEAD_DIM), lambda pair: (0, start + pair))


def attend(image_length, projected):
    return pl.pallas_call(
        attend_kernel,
        grid=(PAIRS,),
        in_specs=[
            pl.BlockSpec(memory_space=pltpu.SMEM),
            column_spec(0),
            column_spec(PAIRS),
            column_spec(2 * PAIRS),
        ],
        out_specs=[
            column_spec(0),
            pl.BlockSpec((1, 2, LONG), lambda pair: (pair, 0, 0)),
        ],
        out_shape=[
            jax.ShapeDtypeStruct((LONG, D), jnp.bfloat16),
            jax.ShapeDtypeStruct((PAIRS, 2, LONG), jnp.float32),
        ],
        compiler_params=pltpu.CompilerParams(vmem_limit_bytes=VMEM),
        cost_estimate=pl.CostEstimate(
            flops=16 * LONG * LONG * D, bytes_accessed=8 * LONG * D, transcendentals=HEADS * LONG * LONG
        ),
        name="attend",
    )(image_length, projected, projected, projected)


def attend_back(image_length, projected, grad_attended, attended, log_total):
    return pl.pallas_call(
        attend_back_kernel,
        grid=(PAIRS,),
        in_specs=[
            pl.BlockSpec(memory_space=pltpu.SMEM),
            column_spec(0),
            column_spec(PAIRS),
            column_spec(2 * PAIRS),
            column_spec(0),
            column_spec(0),
            pl.BlockSpec((1, 2, LONG), lambda pair: (pair, 0, 0)),
        ],
        out_specs=pl.BlockSpec((LONG, 3 * D), lambda pair: (0, 0)),
        out_shape=jax.ShapeDtypeStruct((LONG, 3 * D), jnp.bfloat16),
        scratch_shapes=[pltpu.VMEM((LONG, 2 * HEAD_DIM), jnp.float32)],
        compiler_params=pltpu.CompilerParams(vmem_limit_bytes=VMEM),
        cost_estimate=pl.CostEstimate(
            flops=40 * LONG * LONG * D, bytes_accessed=16 * LONG * D, transcendentals=HEADS * LONG * LONG
        ),
        name="attend_back",
    )(image_length, projected, projected, projected, grad_attended, attended, log_total)


def turn_kernel(rows_ref, turned_ref):
    turned_ref[...] = jnp.transpose(rows_ref[...])


def turn(rows):
    count, wide = rows.shape
    return pl.pallas_call(
        turn_kernel,
        grid=(count // SHORT,),
        in_specs=[pl.BlockSpec((SHORT, wide), lambda i: (i, 0))],
        out_specs=pl.BlockSpec((wide, SHORT), lambda i: (0, i)),
        out_shape=jax.ShapeDtypeStruct((wide, count), rows.dtype),
        cost_estimate=pl.CostEstimate(flops=0, bytes_accessed=4 * count * wide, transcendentals=0),
        name="turn",
    )(rows)


def whole(shape):
    return pl.BlockSpec(shape, lambda *_: (0,) * len(shape), pipeline_mode=pl.Buffered(1))


def gelu_pair(values):
    slope, cubic = math.sqrt(2.0 / math.pi), 0.044715
    square = values * values
    gate = 0.5 + 0.5 * jnp.tanh(values * (slope + slope * cubic * square))
    result = values * gate
    return result, gate + result * (1.0 - gate) * (2.0 * slope + 6.0 * slope * cubic * square)


def ffn_step(rows_ref, grad_ref, w_in_ref, w_out_ref, gelu_ref, pre_ref, out_sum, back_sum, turned_ref, size, turn):
    step = pl.program_id(0)
    count = rows_ref.shape[0]
    w_in = w_in_ref[0]
    w_out = w_out_ref[...].reshape(w_in.shape[1], D)
    for start in range(0, count, size):
        rows = slice(start, start + size)
        pre = product(rows_ref[rows, :], w_in)
        grad_gelu = product_nt(grad_ref[rows, :], w_out)
        value, slope = gelu_pair(pre)
        value = value.astype(jnp.bfloat16)
        grad_pre = (grad_gelu * slope).astype(jnp.bfloat16)
        gelu_ref[rows, :] = value
        pre_ref[rows, :] = grad_pre
        out_sum[rows, :] += product(value, w_out)
        back_sum[rows, :] += product_nt(grad_pre, w_in)
    place = pl.ds(pl.multiple_of(jnp.minimum(step, count // turn - 1) * turn, turn), turn)
    turned_ref[:, place] = jnp.transpose(rows_ref[place, :])


def shared_kernel(rows_ref, grad_ref, w_in_ref, w_out_ref, *refs):
    out_ref, back_ref, gelu_ref, pre_ref, turned_ref = refs[-5:]

    @pl.when(pl.program_id(0) == 0)
    def _():
        out_ref[...] = jnp.zeros_like(out_ref)
        back_ref[...] = jnp.zeros_like(back_ref)

    ffn_step(
        rows_ref, grad_ref, w_in_ref, w_out_ref, gelu_ref, pre_ref, out_ref, back_ref, turned_ref, 256, 256
    )


def below(values):
    values = jnp.concatenate(
        [jnp.broadcast_to(values, (CAP, 128)), jnp.zeros((384 - CAP, 128), jnp.float32)], axis=0
    )
    values = jnp.transpose(values)[:EXTRA]
    first = values.astype(jnp.bfloat16).astype(jnp.float32)
    second = (values - first).astype(jnp.bfloat16).astype(jnp.float32)
    row = lax.broadcasted_iota(jnp.int32, values.shape, 0)
    values = jnp.where(row == 0, first, jnp.where(row == 1, second, values - first - second))
    return jnp.concatenate([values, jnp.zeros((EXTRA, D - 384), jnp.float32)], axis=1).astype(jnp.bfloat16)


def routed_kernel(senders, *refs):
    row_refs, grad_refs, refs = refs[:senders], refs[senders : 2 * senders], refs[2 * senders :]
    w_in_ref, w_out_ref = refs[:2]
    refs = refs[-2 * senders - 8 :]
    out_refs, back_refs = refs[:senders], refs[senders : 2 * senders]
    gelu_ref, pre_ref, weighted_ref, turned_ref, rows_ref, gate_ref, out_sum, back_sum = refs[2 * senders :]
    step, last = pl.program_id(0), pl.num_programs(0) - 1

    @pl.when(step == 0)
    def _():
        out_sum[...] = jnp.zeros_like(out_sum)
        back_sum[...] = jnp.zeros_like(back_sum)
        for k in range(senders):
            rows = slice(k * CAP, (k + 1) * CAP)
            rows_ref[rows, :] = row_refs[k][:CAP, :]
            pieces = row_refs[k][CAP : CAP + EXTRA, :384].astype(jnp.float32)
            gates = pieces[0:1] + pieces[1:2] + pieces[2:3]
            gate_ref[rows, :] = jnp.transpose(jnp.broadcast_to(gates, (128, 384)))[:CAP]
            weighted = gate_ref[rows, 0:1] * grad_refs[k][...].astype(jnp.float32)
            weighted_ref[rows, :] = weighted.astype(jnp.bfloat16)

    ffn_step(
        rows_ref,
        weighted_ref,
        w_in_ref,
        w_out_ref,
        gelu_ref,
        pre_ref,
        out_sum,
        back_sum,
        turned_ref,
        CAP,
        384,
    )

    @pl.when(step == last)
    def _():
        for k in range(senders):
            rows = slice(k * CAP, (k + 1) * CAP)
            result = out_sum[rows, :]
            out_refs[k][...] = (gate_ref[rows, 0:1] * result).astype(jnp.bfloat16)
            back_refs[k][:CAP, :] = back_sum[rows, :].astype(jnp.bfloat16)
            dots = jnp.sum(
                grad_refs[k][...].astype(jnp.float32) * result.astype(jnp.bfloat16).astype(jnp.float32),
                axis=1,
                keepdims=True,
            )
            back_refs[k][CAP:, :] = below(dots)


def ffn_call(kernel, name, operands, specs, w_in, w_out, place, outs, hidden, scratch, width=512, w_specs=None):
    count, ff = outs[hidden].shape
    column = pl.BlockSpec((count, width), lambda step: (0, step))
    out_specs = [column if at in (hidden, hidden + 1) else whole(out.shape) for at, out in enumerate(outs)]
    return pl.pallas_call(
        kernel,
        grid=(ff // width,),
        in_specs=specs
        + (
            w_specs
            or [
                pl.BlockSpec((1, D, width), lambda step: (place, 0, step)),
                pl.BlockSpec((1, width, D), lambda step: (place, step, 0)),
            ]
        ),
        out_specs=out_specs,
        out_shape=outs,
        scratch_shapes=scratch,
        compiler_params=pltpu.CompilerParams(vmem_limit_bytes=VMEM),
        cost_estimate=pl.CostEstimate(
            flops=8 * count * D * ff, bytes_accessed=4 * count * ff + 4 * D * ff, transcendentals=count * ff
        ),
        name=name,
    )(*operands, w_in, w_out)


def shared_expert(rows, grad, w_in, w_out):
    kept = jax.ShapeDtypeStruct((LONG, D), jnp.float32)
    hidden = jax.ShapeDtypeStruct((LONG, w_in.shape[0] * D), jnp.bfloat16)
    turned = jax.ShapeDtypeStruct((D, LONG), jnp.bfloat16)
    full = whole((LONG, D))
    return ffn_call(
        shared_kernel,
        "shared_expert",
        [rows, grad],
        [full, full],
        w_in,
        w_out[0],
        0,
        [kept, kept, hidden, hidden, turned],
        2,
        [],
        D,
        [
            pl.BlockSpec((1, D, D), lambda step: (step, 0, 0)),
            w_out[1] or pl.BlockSpec((1, D, D), lambda step: (0, step, 0)),
        ],
    )


def routed_expert(rows, grads, w_in, w_out, place):
    senders = len(rows)
    count, operands = senders * CAP, list(rows) + list(grads)
    hidden = jax.ShapeDtypeStruct((count, w_in.shape[2]), jnp.bfloat16)
    result = ffn_call(
        lambda *refs: routed_kernel(senders, *refs),
        "routed_expert",
        operands,
        [whole(operand.shape) for operand in operands],
        w_in,
        w_out,
        place,
        [jax.ShapeDtypeStruct((CAP, D), jnp.bfloat16)] * senders
        + [jax.ShapeDtypeStruct((CAP + EXTRA, D), jnp.bfloat16)] * senders
        + [
            hidden,
            hidden,
            jax.ShapeDtypeStruct((count, D), jnp.bfloat16),
            jax.ShapeDtypeStruct((D, count), jnp.bfloat16),
        ],
        2 * senders,
        [
            pltpu.VMEM((count, D), jnp.bfloat16),
            pltpu.VMEM((count, 128), jnp.float32),
            pltpu.VMEM((count, D), jnp.float32),
            pltpu.VMEM((count, D), jnp.float32),
        ],
        768 if count <= 4 * CAP else 512,
    )
    return (result[:senders], result[senders : 2 * senders]) + tuple(result[2 * senders :])


def expert_outer_kernel(added, which_ref, gelu_ref, grad_ref, rows_ref, pre_ref, *refs):
    out_ref, step = refs[-1], pl.program_id(0)
    chips, tall = out_ref.shape[0], gelu_ref.shape[1]
    depth, count = rows_ref.shape[2:]

    @pl.when(step < chips)
    def _():
        result = product_tn(gelu_ref[...], grad_ref[...])
        if added:
            result = result + refs[0][0].astype(jnp.float32)
        out_ref[step, :tall, :] = result.astype(jnp.bfloat16)

    @pl.when(step >= chips)
    def _():
        result = product(rows_ref[...].reshape(chips * depth, count), pre_ref[...])
        result = result.reshape(chips, depth, D)
        place = pl.ds(pl.multiple_of(tall + (step - chips) * depth, 32), depth)
        if added:
            result = result + refs[1][...].astype(jnp.float32)
        out_ref[:, place, :] = result.astype(jnp.bfloat16)


def attention_outer_kernel(added, which_ref, normed_ref, mixed_ref, projected_ref, grad_ref, *refs):
    out_ref, step = refs[-1], pl.program_id(0)
    chips = out_ref.shape[0]
    depth, count = normed_ref.shape[2:]
    place = pl.ds(pl.multiple_of(step * depth, 32), depth)

    def put(left_ref, right_ref):
        result = product(left_ref[...].reshape(chips * depth, count), right_ref[...])
        result = result.reshape(chips, depth, D)
        if added:
            result = result + refs[0][:, place, :].astype(jnp.float32)
        out_ref[:, place, :] = result.astype(jnp.bfloat16)

    @pl.when(step < 3)
    def _():
        put(normed_ref, projected_ref)

    @pl.when(step == 3)
    def _():
        put(mixed_ref, grad_ref)


def outer_call(kernel, name, steps, which, operands, specs, rows, came, came_specs, tokens, flops):
    chips = lax.axis_size("dp") // 2
    full = whole((chips, rows, D))
    extra = [] if came is None else [came] * len(came_specs or [full])
    return pl.pallas_call(
        lambda *refs: kernel(came is not None, *refs),
        grid_spec=pltpu.PrefetchScalarGridSpec(
            num_scalar_prefetch=1,
            grid=(steps,),
            in_specs=specs + (came_specs or [full])[: len(extra)] + [HBM] * len(tokens),
            out_specs=full,
        ),
        out_shape=jax.ShapeDtypeStruct((chips, rows, D), jnp.bfloat16),
        compiler_params=pltpu.CompilerParams(vmem_limit_bytes=VMEM),
        cost_estimate=pl.CostEstimate(
            flops=flops,
            bytes_accessed=sum(2 * operand.size for operand in operands) + 4 * chips * rows * D,
            transcendentals=0,
        ),
        name=name,
    )(jnp.reshape(which, (1,)).astype(jnp.int32), *operands, *extra, *tokens)


def by_device(turned):
    n_dp = lax.axis_size("dp")
    return turned.reshape(n_dp // 2, 2, turned.shape[0] // n_dp, turned.shape[1])


def plain_outer(pairs):
    n_dp = lax.axis_size("dp")

    def make(which, came, tokens):
        parts = []
        for turned, right in pairs:
            result = product(turned, right).reshape(n_dp // 2, 2, turned.shape[0] // n_dp, right.shape[1])
            result = at_place(result, which, 1).reshape(n_dp // 2, -1, right.shape[1] // D, D)
            parts.append(jnp.swapaxes(result, 1, 2).reshape(n_dp // 2, -1, D))
        parts = jnp.concatenate(parts, axis=1)
        parts = parts if came is None else parts + came.astype(jnp.float32)
        return parts.astype(jnp.bfloat16)

    return make


def expert_outer(gelu, grad, turned, grad_pre):
    n_dp, (count, ff) = lax.axis_size("dp"), gelu.shape
    chips, tall, depth = n_dp // 2, ff // n_dp, D // n_dp
    if tall % 128 or depth % 32:
        return plain_outer([(jnp.swapaxes(gelu, 0, 1), grad), (turned, grad_pre)])
    turned = by_device(turned)
    specs = [
        pl.BlockSpec((count, tall), lambda i, which: (0, 2 * jnp.minimum(i, chips - 1) + which[0])),
        whole((count, D)),
        pl.BlockSpec((chips, 1, depth, count), lambda i, which: (0, which[0], 0, 0)),
        pl.BlockSpec((count, D), lambda i, which: (0, jnp.maximum(i - chips, 0))),
    ]
    return lambda which, came, tokens: outer_call(
        expert_outer_kernel,
        "expert_outer",
        chips + ff // D,
        which,
        [gelu, grad, turned, grad_pre],
        specs,
        tall + ff // D * depth,
        came,
        [
            pl.BlockSpec((1, tall, D), lambda i, which: (jnp.minimum(i, chips - 1), 0, 0)),
            pl.BlockSpec(
                (chips, depth, D), lambda i, which: (0, tall // depth + jnp.maximum(i - chips, 0), 0)
            ),
        ],
        tokens,
        2 * count * D * ff,
    )


def attention_outer(left, grad_projected, grad_att):
    n_dp = lax.axis_size("dp")
    chips, depth = n_dp // 2, D // n_dp
    if depth % 32:
        return plain_outer([(left[0], grad_projected), (left[1], grad_att)])
    own = pl.BlockSpec((chips, 1, depth, LONG), lambda i, which: (0, which[0], 0, 0))
    specs = [
        own,
        own,
        pl.BlockSpec((LONG, D), lambda i, which: (0, jnp.minimum(i, 2))),
        whole((LONG, D)),
    ]
    operands = [by_device(left[0]), by_device(left[1]), grad_projected, grad_att]
    return lambda which, came, tokens: outer_call(
        attention_outer_kernel,
        "attention_outer",
        4,
        which,
        operands,
        specs,
        4 * depth,
        came,
        None,
        tokens,
        4 * LONG * D * D,
    )


def to_core(make, tokens=()):
    return make(1 - lax.axis_index("dp") % 2, None, list(tokens))


def from_core(sent):
    return lax.ppermute(sent, "dp", [(i, i ^ 1) for i in range(lax.axis_size("dp"))])


def with_core(make, came, tokens=()):
    return make(lax.axis_index("dp") % 2, came, list(tokens))


def combine_kernel(count, dotted, ids_ref, slots_ref, base_ref, *refs):
    block_refs, refs = refs[:count], refs[count:]
    out_ref, dots_out_ref, rows_ref, dots_ref = refs
    size = block_refs[0].shape[0]

    @pl.when(pl.program_id(0) == 0)
    def _():
        for at, block_ref in enumerate(block_refs):
            rows_ref[at * size : (at + 1) * size, :] = block_ref[...]
            if dotted:
                pieces = block_ref[CAP:, :size].astype(jnp.float32)
                dots_ref[:, at * size : (at + 1) * size] = pieces[0:1] + pieces[1:2] + pieces[2:3]

    ids = ids_ref[...]
    first, second = slots_ref[:, 0:1] == ids, slots_ref[:, 1:2] == ids
    hold = jnp.where(first | second, 1.0, 0.0).astype(jnp.bfloat16)
    out_ref[...] = base_ref[...] + product(hold, rows_ref[...])
    if dotted:
        dots = dots_ref[...]
        dots_out_ref[:, 0:1] = jnp.sum(jnp.where(first, dots, 0.0), axis=1, keepdims=True)
        dots_out_ref[:, 1:2] = jnp.sum(jnp.where(second, dots, 0.0), axis=1, keepdims=True)


def combine(ids, slots, base, blocks, dotted):
    total = ids.shape[1]
    patch = pl.BlockSpec((SHORT, D), lambda i: (i, 0))
    pair = pl.BlockSpec((SHORT, 2), lambda i: (i, 0))
    return pl.pallas_call(
        lambda *refs: combine_kernel(len(blocks), dotted, *refs),
        grid=(BLOCKS,),
        in_specs=[whole(ids.shape), pair, patch] + [whole(block.shape) for block in blocks],
        out_specs=[patch, pair],
        out_shape=[
            jax.ShapeDtypeStruct((LONG, D), jnp.float32),
            jax.ShapeDtypeStruct((LONG, 2), jnp.float32),
        ],
        scratch_shapes=[pltpu.VMEM((total, D), jnp.bfloat16), pltpu.VMEM((1, total), jnp.float32)],
        compiler_params=pltpu.CompilerParams(vmem_limit_bytes=VMEM),
        cost_estimate=pl.CostEstimate(
            flops=2 * LONG * total * D, bytes_accessed=2 * total * D + 8 * LONG * D, transcendentals=0
        ),
        name="combine",
    )(ids, slots, base, *blocks)


def sums_kernel(groups, *refs):
    out_ref, in_ref = refs[-2:]
    depth, wide = in_ref.shape[1:]
    expert, step = pl.program_id(0), pl.program_id(1)
    start = 0
    for at, count in enumerate(groups):
        parts = refs[start : start + count]
        start += count

        @pl.when(expert == at)
        def _(parts=parts):
            total = parts[0][...].astype(jnp.float32)
            for part in parts[1:]:
                total = total + part[...].astype(jnp.float32)

            @pl.when(step == 0)
            def _():
                out_ref[0] = total

            @pl.when(step == 1)
            def _():
                for j in range(wide // D):
                    in_ref[0, :, j * D : (j + 1) * D] = total[j * depth : (j + 1) * depth, :]


def expert_sums(pieces, tall, depth, wide):
    count = len(pieces)

    def spec(at, row):
        def index(expert, step):
            return row // tall + jnp.where(expert == at, step, 0 if at else 1), 0

        return pl.BlockSpec((tall, D), index)

    return pl.pallas_call(
        lambda *refs: sums_kernel([len(group) for group in pieces], *refs),
        grid=(count, 2),
        in_specs=[spec(at, row) for at, group in enumerate(pieces) for _, row in group],
        out_specs=[
            pl.BlockSpec((1, tall, D), lambda expert, step: (expert, 0, 0)),
            pl.BlockSpec((1, depth, wide), lambda expert, step: (expert, 0, 0)),
        ],
        out_shape=[
            jax.ShapeDtypeStruct((count, tall, D), jnp.float32),
            jax.ShapeDtypeStruct((count, depth, wide), jnp.float32),
        ],
        compiler_params=pltpu.CompilerParams(vmem_limit_bytes=VMEM),
        cost_estimate=pl.CostEstimate(
            flops=0, bytes_accessed=32 * count * tall * D, transcendentals=0
        ),
        name="expert_sums",
    )(*[array for group in pieces for array, _ in group])


def dispatch_kernel(count, ids_ref, slots_ref, gates_ref, rows_ref, *out_refs):
    size = ids_ref.shape[0] // count
    for at, out_ref in enumerate(out_refs):
        ids = ids_ref[at * size : (at + 1) * size, :]
        first, second = slots_ref[0:1, :] == ids, slots_ref[1:2, :] == ids
        hold = jnp.where(first | second, 1.0, 0.0).astype(jnp.bfloat16)
        out_ref[:CAP, :] = product(hold, rows_ref[...])[:CAP].astype(jnp.bfloat16)
        gates = jnp.where(first, gates_ref[0:1, :], 0.0) + jnp.where(second, gates_ref[1:2, :], 0.0)
        out_ref[CAP:, :] = below(jnp.sum(gates, axis=1, keepdims=True)[:CAP])


def dispatch(ids, slots, gates, rows, count):
    size = ids.shape[0] // count
    return pl.pallas_call(
        lambda *refs: dispatch_kernel(count, *refs),
        out_shape=[jax.ShapeDtypeStruct((size, D), jnp.bfloat16)] * count,
        compiler_params=pltpu.CompilerParams(vmem_limit_bytes=VMEM),
        cost_estimate=pl.CostEstimate(
            flops=2 * LONG * ids.shape[0] * D, bytes_accessed=2 * (LONG + ids.shape[0]) * D, transcendentals=0
        ),
        name="dispatch",
    )(ids, slots, gates, rows)


def gather_kernel(n_dp, n_ex, own_ref, all_ref, here_sem, z_out, z_in, chip_out, chip_in, core_out, core_in):
    dp, ex = lax.axis_index("dp"), lax.axis_index("expert")
    chips = n_dp // 2

    def along(axis, distance):
        if axis == "expert":
            return (dp, ex ^ distance)
        return (dp ^ distance, ex)

    routes = (
        [("expert", k) for k in range(1, n_ex)] + [("dp", 2 * k) for k in range(1, chips)] + [("dp", 1)]
    )
    barrier = pltpu.get_barrier_semaphore()
    for route in routes:
        pl.semaphore_signal(barrier, inc=1, device_id=along(*route), device_id_type=pl.DeviceIdType.MESH)
    pl.semaphore_wait(barrier, len(routes))

    def send(source, target, sent, came, device):
        copy = pltpu.make_async_remote_copy(
            src_ref=source,
            dst_ref=target,
            send_sem=sent,
            recv_sem=came,
            device_id=device,
            device_id_type=pl.DeviceIdType.MESH,
        )
        copy.start()
        return copy

    def wait_for(target, came):
        pltpu.make_async_remote_copy(
            src_ref=target,
            dst_ref=target,
            send_sem=came,
            recv_sem=came,
            device_id=(dp, ex),
            device_id_type=pl.DeviceIdType.MESH,
        ).wait_recv()

    def group(device, first=0, count=n_ex):
        return all_ref.at[pl.ds(device * n_ex + first, count)]

    mine = all_ref.at[dp * n_ex + ex]
    here = pltpu.make_async_copy(own_ref, mine, here_sem)
    here.start()
    sends = [
        send(own_ref, mine, z_out.at[k], z_in.at[k], along("expert", k)) for k in range(1, n_ex)
    ]
    for k in range(1, n_ex):
        wait_for(all_ref.at[dp * n_ex + (ex ^ k)], z_in.at[k])
    here.wait()
    direct = [1, 2] if chips == 4 else list(range(1, chips))
    for k in direct:
        sends.append(send(group(dp), group(dp), chip_out.at[k], chip_in.at[k], along("dp", 2 * k)))
    sends.append(send(group(dp), group(dp), core_out.at[0], core_in.at[0], along("dp", 1)))
    for k in direct:
        other = dp ^ (2 * k)
        wait_for(group(other), chip_in.at[k])
        if chips == 4:
            part = group(other, (k - 1) * (n_ex // 2), n_ex // 2)
            sends.append(send(part, part, chip_out.at[2 + k], chip_in.at[2 + k], along("dp", 2 * (3 - k))))
        sends.append(send(group(other), group(other), core_out.at[k], core_in.at[k], along("dp", 1)))
    if chips == 4:
        other = dp ^ 6
        for k in direct:
            wait_for(group(other, (k - 1) * (n_ex // 2), n_ex // 2), chip_in.at[2 + k])
        sends.append(send(group(other), group(other), core_out.at[3], core_in.at[3], along("dp", 1)))
    for k in range(chips):
        wait_for(group(dp ^ (2 * k) ^ 1), core_in.at[k])
    for copy in sends:
        copy.wait_send()


def gather(own):
    n_dp, n_ex = lax.axis_size("dp"), lax.axis_size("expert")
    chips = n_dp // 2
    counts = (n_ex, n_ex, max(chips, 5), max(chips, 5), chips, chips)
    return pl.pallas_call(
        lambda *refs: gather_kernel(n_dp, n_ex, *refs),
        in_specs=[HBM],
        out_specs=HBM,
        out_shape=jax.ShapeDtypeStruct((n_dp * n_ex,) + own.shape, own.dtype),
        scratch_shapes=[pltpu.SemaphoreType.DMA] + [pltpu.SemaphoreType.DMA((count,)) for count in counts],
        compiler_params=pltpu.CompilerParams(collective_id=0, has_side_effects=True),
        cost_estimate=pl.CostEstimate(flops=0, bytes_accessed=64 * own.size, transcendentals=0),
        name="gather",
    )(own)


def swap(parts, axis):
    return lax.all_to_all(parts, axis, 0, 0, tiled=True)


def at_place(parts, place, axis=0):
    return lax.dynamic_index_in_dim(parts, place, axis, keepdims=False)


def from_expert(parts):
    size, me = parts.shape[0], lax.axis_index("expert")
    arrived = [at_place(parts, me)]
    for distance in range(1, size):
        route = [(i, i ^ distance) for i in range(size)]
        arrived.append(lax.ppermute(at_place(parts, me ^ distance), "expert", route))
    return arrived


def together(live, work, *operands):
    def never(*operands):
        return jax.tree.map(lambda out: jnp.zeros(out.shape, out.dtype), jax.eval_shape(work, *operands))

    return lax.cond(live, work, never, *operands)


def to_expert(blocks, distances=None):
    size = len(blocks)
    return [
        lax.ppermute(blocks[distance], "expert", [(i, i ^ distance) for i in range(size)])
        if distance
        else blocks[0]
        for distance in (range(size) if distances is None else distances)
    ]


def from_chips(parts, distances):
    chips, me = lax.axis_size("dp") // 2, lax.axis_index("dp") // 2
    arrived = []
    for distance in distances if parts else []:
        route = [(i, i ^ (2 * distance)) for i in range(2 * chips)]
        part = jnp.concatenate([at_place(array, me ^ distance) for array in parts], axis=0)
        arrived.append(lax.ppermute(part, "dp", route) if distance else part)
    return arrived


def total_of(arrived):
    total = arrived[0].astype(jnp.float32)
    for part in arrived[1:]:
        total = total + part.astype(jnp.float32)
    return total


def body(
    tokens,
    bucket,
    image_length,
    routes,
    cotangent,
    w_qkv,
    w_out,
    w_ada,
    b_ada,
    w_router,
    w_shared_in,
    w_shared_out,
    w_expert_in,
    w_expert_out,
):
    n_dp, n_ex = lax.axis_size("dp"), lax.axis_size("expert")
    n, chips = n_dp * n_ex, n_dp // 2
    dp = lax.axis_index("dp")
    share = D // n
    ff = w_shared_in.shape[1]
    wide = w_ada.shape[1]
    column = wide // n

    ada_parts = jnp.swapaxes(w_ada.reshape(share, n, column), 0, 1)
    bucket_row = jnp.zeros((1, 1, column), jnp.bfloat16).at[0, 0, :BLOCKS].set(bucket.astype(jnp.bfloat16))
    ada_parts = jnp.concatenate([ada_parts, jnp.broadcast_to(bucket_row, (n, 1, column))], axis=1)
    ada_parts = swap(ada_parts, BOTH)
    ada_columns = ada_parts[:, :share].reshape(D, column)
    buckets = ada_parts[:, share, :BLOCKS].astype(jnp.int32).reshape(n * BLOCKS)
    condition = jax.nn.silu(embed(buckets)).astype(jnp.bfloat16)
    modulation = product(condition, ada_columns) + b_ada.astype(jnp.float32)
    w_qkv = w_qkv + (0.0 * modulation[0, 0]).astype(jnp.bfloat16)
    modulation = swap(modulation.reshape(n, BLOCKS, column), BOTH)
    modulation = jnp.swapaxes(modulation, 0, 1).reshape(BLOCKS, wide)

    def span(index):
        return expand(modulation[:, index * D : (index + 1) * D])

    shift_one, scale_one, gate_one, shift_two, scale_two, gate_two = [span(index) for index in range(6)]

    w_qkv = gather(w_qkv).reshape(D, 3 * D)
    router_rows = jnp.zeros((8, D), jnp.bfloat16).at[0, : share * EXPERTS].set(w_router.reshape(-1))
    packed = jnp.concatenate(
        [w_shared_out, w_out]
        + [w_shared_in[:, at * D : (at + 1) * D] for at in range(ff // D)]
        + [router_rows],
        axis=0,
    )
    packed = lax.all_gather(packed, BOTH, axis=0, tiled=False)
    start = ff // n
    w_out = packed[:, start : start + share].reshape(D, D)
    w_shared_in = packed[:, start + share : start + (1 + ff // D) * share].reshape(n, ff // D, share, D)
    w_shared_in = jnp.swapaxes(w_shared_in, 0, 1).reshape(ff // D, D, D)
    w_router = packed[:, start + (1 + ff // D) * share, : share * EXPERTS].reshape(D, EXPERTS)
    if start % 16 == 0:
        w_shared_out = packed, pl.BlockSpec((D // start, start, D), lambda step: (step, 0, 0))
    else:
        w_shared_out = packed[:, :start].reshape(1, ff, D), None

    choose = [routes[:, k : k + 1] == jnp.arange(EXPERTS, dtype=jnp.int32)[None, :] for k in range(2)]
    named = (choose[0] | choose[1]).astype(jnp.bfloat16)
    position = jnp.arange(LONG, dtype=jnp.int32)
    earlier = (position[:, None] > position[None, :]).astype(jnp.bfloat16)
    before = product(earlier, named)
    slots = [
        routes[:, k] * CAP + jnp.sum(jnp.where(choose[k], before, 0.0), axis=1).astype(jnp.int32)
        for k in range(2)
    ]
    local = EXPERTS // n_ex
    ex = lax.axis_index("expert")
    near = jnp.stack([ex ^ k for k in range(n_ex)]).astype(jnp.int32)

    def slot_ids(which, size):
        place = jnp.arange(size, dtype=jnp.int32)
        experts = jnp.asarray(which, jnp.int32)[:, None] + near[None, :] * local
        return jnp.where(place < CAP, (experts * CAP)[:, :, None] + place, -1).reshape(-1)

    def hold(at, size):
        ids = slot_ids([at], size)[:, None]
        return ((ids == slots[0][None, :]) | (ids == slots[1][None, :])).astype(jnp.bfloat16)

    slot_pairs = jnp.stack(slots, axis=1)

    grad_out = cotangent.astype(jnp.float32)
    grad_mlp = (gate_two * grad_out).astype(jnp.bfloat16)

    def grad_blocks(at, grad_mlp):
        blocks = product(hold(at, CAP), grad_mlp).astype(jnp.bfloat16).reshape(n_ex, CAP, D)
        return [blocks[k] for k in range(n_ex)]

    grad_sent = grad_blocks(0, grad_mlp)
    live = image_length[0] > 0

    inputs_full = tokens.astype(jnp.float32)
    hat_one, inverse_one = normalize(inputs_full)
    normed_one = (hat_one * (1.0 + scale_one) + shift_one).astype(jnp.bfloat16)
    projected = product(normed_one, w_qkv).astype(jnp.bfloat16)
    def attention_part(projected, blocks, grad_mlp):
        others = [grad_blocks(at, grad_mlp) for at in range(1, local)]
        return *attend(image_length, projected), to_expert(blocks), others

    attended, log_total, grad_rows, grad_sent = together(
        live, attention_part, projected, grad_sent, grad_mlp
    )
    grad_rows = [grad_rows]
    branch_att = product(attended, w_out)
    hidden_one = inputs_full + gate_one * branch_att
    hat_two, inverse_two = normalize(hidden_one)
    normed_two = (hat_two * (1.0 + scale_two) + shift_two).astype(jnp.bfloat16)

    logits = product(normed_two, w_router)
    picked_logits = jnp.stack([jnp.sum(jnp.where(pick, logits, 0.0), axis=-1) for pick in choose], axis=-1)
    gate_weights = jax.nn.softmax(picked_logits, axis=-1)
    full = CAP + EXTRA

    blocks = dispatch(
        slot_ids(range(local), full)[:, None],
        jnp.stack(slots),
        jnp.swapaxes(gate_weights, 0, 1),
        normed_two,
        local * n_ex,
    )
    sent = [blocks[at * n_ex : (at + 1) * n_ex] for at in range(local)]

    tall = ff // n_dp
    size = tall + ff // D * (D // n_dp)
    near_chips, far_chips = list(range(min(3, chips))), list(range(3, chips))

    def split_expert(part):
        blocks = jnp.swapaxes(part[tall:].reshape(ff // D, D // n_dp, D), 0, 1)
        return part[:tall], blocks.reshape(D // n_dp, ff)

    pieces = [[] for _ in range(1 + local)]

    def note(arrays, *which):
        for row, at in enumerate(which):
            pieces[at] += [(array, row * size) for array in arrays]

    def sum_of(at):
        return total_of([array[row : row + size] for array, row in pieces[at]])

    def first_part(normed_two, grad_mlp, blocks):
        results = shared_expert(normed_two, grad_mlp, w_shared_in, w_shared_out)
        half = to_core(expert_outer(results[2], grad_mlp, results[4], results[3]))
        return results, half, to_expert(blocks)

    results, shared_half, arrived = together(live, first_part, normed_two, grad_mlp, sent[0])
    shared, grad_normed_two, gelu_shared, grad_pre_shared, turned_shared = results

    def second_part(rows, grads, others):
        results = routed_expert(rows, grads, w_expert_in, w_expert_out, 0)
        half = to_core(expert_outer(results[2], results[4], results[5], results[3]))
        return results, half, [to_expert(blocks) for blocks in others]

    def weights_part(gelu, weighted, turned, grad_pre, half, shared_half, grads):
        came = [from_core(half), from_core(shared_half)]
        kept = [with_core(expert_outer(gelu, weighted, turned, grad_pre), came[0])]
        make = expert_outer(gelu_shared, grad_mlp, turned_shared, grad_pre_shared)
        kept.append(with_core(make, came[1], kept))
        return kept, [to_expert(blocks) for blocks in grads]

    results, half, others = together(live, second_part, arrived, grad_rows[0], sent[1:])
    outs, backs, gelu, grad_pre, weighted, turned_rows = results
    arrived = [arrived] + others
    (kept_first, kept_shared), others = together(
        live, weights_part, gelu, weighted, turned_rows, grad_pre, half, shared_half, grad_sent
    )
    grad_rows += others
    out_rows, grad_home, kept_last = [outs], [], []

    def third_part(rows, grads, at, backs, kept):
        results = routed_expert(rows, grads, w_expert_in, w_expert_out, at)
        half = to_core(expert_outer(results[2], results[4], results[5], results[3]))
        return results, half, to_expert(backs), from_chips(kept, near_chips)

    def fourth_part(gelu, weighted, turned, grad_pre, half, backs, kept):
        kept_now = with_core(expert_outer(gelu, weighted, turned, grad_pre), from_core(half))
        return kept_now, to_expert(backs), from_chips(kept, far_chips), [turn(normed_one), turn(attended)]

    if local == 1:
        turned = [turn(normed_one), turn(attended)]
        backs = to_expert(backs)
        note(from_chips([kept_first], near_chips), 0)
        note(from_chips([kept_shared], near_chips + far_chips), 1)
    for at in range(1, local):
        results, half, home, part = together(
            live,
            lambda rows, grads, backs, kept, at=at: third_part(rows, grads, at, backs, kept),
            arrived[at],
            grad_rows[at],
            backs,
            [kept_first, kept_shared] if at == 1 else kept_last[-1:],
        )
        note(part, *((0, 1) if at == 1 else (at,)))
        outs, backs, gelu, grad_pre, weighted, turned_rows = results
        out_rows.append(outs)
        grad_home.append(home)
        kept_now, backs, part, turned = together(
            live,
            fourth_part,
            gelu,
            weighted,
            turned_rows,
            grad_pre,
            half,
            backs,
            [kept_shared] if at == 1 else kept_last[-1:],
        )
        note(part, 1 if at == 1 else at)
        kept_last.append(kept_now)
    grad_home.append(backs)

    def fifth_part(grad_normed_two, grad_home, others, kept):
        ids = slot_ids(range(local), full)[None, :]
        grad_normed_two, grad_gates = combine(ids, slot_pairs, grad_normed_two, sum(grad_home, []), True)
        grad_picked = gate_weights * (
            grad_gates - jnp.sum(gate_weights * grad_gates, axis=1, keepdims=True)
        )
        grad_logits = jnp.where(choose[0], grad_picked[:, 0:1], 0.0) + jnp.where(
            choose[1], grad_picked[:, 1:2], 0.0
        )
        logit_parts = jnp.concatenate(split_three(grad_logits), axis=1).astype(jnp.bfloat16)
        grad_router = product_tn(normed_two, logit_parts).reshape(D, 3, EXPERTS).sum(axis=1)
        grad_normed_two = grad_normed_two + product_nt(
            logit_parts, jnp.concatenate([w_router, w_router, w_router], axis=1)
        )

        grad_hidden_one = cotangent.astype(jnp.float32) + norm_back(
            grad_normed_two * (1.0 + span(4)), hat_two, inverse_two
        )
        grad_att = (span(2) * grad_hidden_one).astype(jnp.bfloat16)
        grad_attended = product_nt(grad_att, w_out).astype(jnp.bfloat16)
        grad_spans = [
            block_sums(grad_hidden_one * product(attended, w_out)),
            block_sums(grad_normed_two),
            block_sums(grad_normed_two * hat_two),
        ]
        results = (grad_router, grad_spans, grad_hidden_one, grad_att, grad_attended)
        return results, [to_expert(blocks) for blocks in others], from_chips(kept, near_chips)

    results, returned, part = together(
        live, fifth_part, grad_normed_two, grad_home, out_rows[:-1], kept_last[-1:]
    )
    grad_router, grad_spans, grad_hidden_one, grad_att, grad_attended = results
    note(part, local)

    def sixth_part(projected, grad_attended, attended, log_total, blocks, kept):
        result = attend_back(image_length, projected, grad_attended, attended, log_total)
        half = to_core(attention_outer(turned, result, grad_att))
        grad_shared_out, grad_shared_in = split_expert(sum_of(1).astype(jnp.bfloat16))
        rows = (D // n_dp) * (ff // n_ex) // D
        shared_parts = jnp.concatenate(
            [
                jnp.swapaxes(grad_shared_in.reshape(D // n_dp, n_ex, ff // n_ex), 0, 1).reshape(
                    n_ex, rows, D
                ),
                jnp.swapaxes(grad_shared_out.reshape(ff // n_dp, n_ex, D // n_ex), 0, 1).reshape(
                    n_ex, rows, D
                ),
            ],
            axis=1,
        )
        return result, half, to_expert(blocks), from_chips(kept, far_chips), shared_parts

    grad_projected, half, rows, part, shared_parts = together(
        live,
        sixth_part,
        projected,
        grad_attended,
        attended,
        log_total,
        out_rows[-1],
        [kept_first] + kept_last[-1:],
    )
    note(part, *([0, local] if local > 1 else [0]))
    returned.append(rows)

    def seventh_part(grad_projected, half, shared_parts):
        came = from_core(half)
        grad_normed_one = product_nt(grad_projected, w_qkv)
        hat_one, inverse_one = normalize(tokens.astype(jnp.float32))
        grad_input = grad_hidden_one + norm_back(
            grad_normed_one * (1.0 + span(1)), hat_one, inverse_one
        )
        spans = [block_sums(grad_normed_one), block_sums(grad_normed_one * hat_one)]
        kept = with_core(attention_outer(turned, grad_projected, grad_att), came)
        return grad_input.astype(jnp.bfloat16), spans, kept, from_expert(shared_parts)

    grad_input, spans, kept, shared_parts = together(
        live, seventh_part, grad_projected, half, shared_parts
    )

    def eighth_part(kept, returned):
        arrived = from_chips([kept], list(range(chips)))
        routed = [group for at, group in enumerate(pieces) if at != 1]
        grad_expert_out, grad_expert_in = expert_sums(routed, tall, D // n_dp, ff)
        ids = slot_ids(range(local), CAP)[None, :]
        branch_mlp = combine(ids, slot_pairs, shared, sum(returned, []), False)[0]
        result = hidden_one + span(5) * branch_mlp
        last_span = block_sums(cotangent.astype(jnp.float32) * branch_mlp)
        return arrived, grad_expert_out, grad_expert_in, result.astype(jnp.bfloat16), last_span

    attention_parts, grad_expert_out, grad_expert_in, result, last_span = together(
        live, eighth_part, kept, returned
    )
    grad_modulation = jnp.concatenate(spans + grad_spans + [last_span], axis=1)

    own_wide, router_rows, router_columns = wide // n_ex, D // n_dp, EXPERTS // n_ex
    by_expert = jnp.swapaxes(grad_modulation.reshape(BLOCKS, n_ex, own_wide), 0, 1)
    message = jnp.concatenate(
        [
            jnp.broadcast_to(
                by_expert.reshape(1, n_ex, BLOCKS * own_wide), (n_dp, n_ex, BLOCKS * own_wide)
            ),
            jnp.sum(grad_modulation, axis=0).reshape(n_dp, n_ex, column),
            jnp.swapaxes(grad_router.reshape(n_dp, router_rows, n_ex, router_columns), 1, 2).reshape(
                n_dp, n_ex, router_rows * router_columns
            ),
        ],
        axis=2,
    )
    length = message.shape[2]
    message = jnp.pad(message.astype(jnp.bfloat16), ((0, 0), (0, 0), (0, -length % 128))).reshape(n, -1, 128)
    message = swap(message, BOTH).reshape(n, -1).astype(jnp.float32)
    at = BLOCKS * own_wide
    every_modulation = message[:, :at].reshape(n * BLOCKS, own_wide)
    grad_b_ada = jnp.sum(message[:, at : at + column], axis=0)
    grad_router = jnp.sum(message[:, at + column : length], axis=0).reshape(router_rows, router_columns)
    own_condition = lax.dynamic_slice_in_dim(condition, dp * (D // n_dp), D // n_dp, axis=1)

    attention_parts = total_of(attention_parts).astype(jnp.bfloat16).reshape(4, D // n_dp, D)
    attention_parts = jnp.concatenate(
        [
            jnp.swapaxes(attention_parts[:3], 0, 1).reshape(D // n_dp, n_ex, 3 * D // n_ex),
            attention_parts[3].reshape(D // n_dp, n_ex, D // n_ex),
        ],
        axis=2,
    )
    rest = (D // n_dp) * 4 // n_ex
    attention_parts = jnp.swapaxes(attention_parts, 0, 1).reshape(n_ex, rest, D)

    parts = together(live, from_expert, attention_parts)
    grad_w_ada = lax.dot_general(
        own_condition.astype(jnp.float32),
        every_modulation,
        (((0,), (0,)), ((), ())),
        precision=HIGHEST,
        preferred_element_type=jnp.float32,
    )
    attention_parts = total_of(parts).reshape(D // n_dp, 4 * D // n_ex)
    shared_parts = total_of(shared_parts)
    half = shared_parts.shape[0] // 2
    return (
        result,
        grad_input,
        attention_parts[:, : 3 * D // n_ex],
        attention_parts[:, 3 * D // n_ex :],
        grad_w_ada,
        grad_b_ada,
        grad_router,
        shared_parts[:half].reshape(D // n_dp, ff // n_ex),
        shared_parts[half:].reshape(ff // n_dp, D // n_ex),
        grad_expert_in,
        grad_expert_out,
    )


def solution(mesh):
    rows, flat = P(BOTH, None), P(BOTH)
    spread = P("dp", "expert")
    return jax.shard_map(
        body,
        mesh=mesh,
        in_specs=(
            rows,
            flat,
            flat,
            rows,
            rows,
            rows,
            rows,
            rows,
            flat,
            rows,
            rows,
            rows,
            P("expert", None, None),
            P("expert", None, None),
        ),
        out_specs=(
            rows,
            rows,
            spread,
            spread,
            spread,
            flat,
            spread,
            spread,
            spread,
            P("expert", "dp", None),
            P("expert", "dp", None),
        ),
        check_vma=False,
    )
```
